32 devices in a mesh: ctx: 8 (over y, x, core), grp: 4 (over z).
Axes of the slice: x: 2, y: 2, z: 4, core: 2. Of those that a mesh axis runs over, the one named last changes fastest.
Arguments:
- q_latent: bfloat16 [8, 128, 512], P('grp', 'ctx'), parts along dimension 0, may hold values from -48 to 48
- q_rope: bfloat16 [8, 128, 64], P('grp', 'ctx'), parts along dimension 0, may hold values from -48 to 48
- latent_cache: bfloat16 [256, 64, 576], P(('grp', 'ctx')), parts along dimension 0, may hold values from -6 to 6
- page_table: int32 [8, 32], P('grp'), parts along dimension 0, may hold values from 0 to 63, as said below
- lengths: int32 [8], P('grp'), parts along dimension 0, may hold values from 1 to 2048, 2560 in all
- w_uv: bfloat16 [128, 512, 128], P('ctx'), may hold values from -6 to 6
- w_out: bfloat16 [16384, 7168], P('ctx'), may hold values from -0.046875 to 0.046875
Outputs:
- layer_out: bfloat16 [8, 7168], P('grp'), parts along dimension 0
The draws below stay inside these ranges and needn't reach their ends.
There are 4 independent parts, one for each index of `grp`. The reference program is written for one: setup_inputs(seed, part) draws one part's arguments, and reference() takes and returns one part's arrays. A program takes and returns all parts, laid end to end along the dimension named above; an argument that names none is the same for every part. Nothing has to cross between parts.
Inputs may be any that keep to these rules, and one draw needn't show every extreme that they name: `page_table`: every page number stands exactly once in the table. The longest row is at most 2048; all lengths sum to 2560.
All inputs are finite; a program needn't handle non-finite values.
Results may differ from the reference program's by a relative error of at most 0.03.
Values may be sent and summed in bfloat16 or wider, within the bound.
A program may use at most 128 MiB of HBM per device.

```python
import math
import jax
import jax.numpy as jnp
import numpy as np
from jax import lax

H = 128
C = 512
ROPE = 64
V = 128
D = 7168
PAGE = 64
ROWS = 2
PAGES = 64
MAXP = 32


def page_order(key):
    order = jax.random.permutation(jax.random.fold_in(key, 7), PAGES)
    return order.astype(jnp.int32).reshape(ROWS, MAXP)


def cache_base(key):
    base = jax.random.normal(jax.random.fold_in(key, 11), (PAGES, PAGE, C + ROPE), jnp.float32)
    return jnp.clip(base, -6.0, 6.0)


def query_full(key, strength):
    base = jnp.clip(jax.random.normal(jax.random.fold_in(key, 13), (ROWS, H, C + ROPE), jnp.float32), -6.0, 6.0)
    chosen = (jnp.arange(H) % 8 == 0).astype(jnp.float32) * jnp.float32(strength)
    return base * (1.0 - chosen[None, :, None])


def draw_page_table(key, part):
    table = page_order(key)
    return table


def draw_latent_cache(key, part):
    base = cache_base(key)
    return base.astype(jnp.bfloat16)


def draw_q_latent(key, part):
    strength = 0.0
    full = query_full(key, strength)
    return full[:, :, :C].astype(jnp.bfloat16)


def draw_q_rope(key, part):
    strength = 0.0
    full = query_full(key, strength)
    return full[:, :, C:].astype(jnp.bfloat16)


def level_of(stream_key, dims, shards, low, high):
    level = 1.0
    for dim, blocks in shards:
        draws = jax.random.uniform(jax.random.fold_in(jax.random.fold_in(stream_key, 6), dim), (blocks,), jnp.float32, low / len(shards), high / len(shards))
        level = level * jnp.repeat(jnp.exp(draws), dims[dim] // blocks).reshape((-1,) + (1,) * (len(dims) - 1 - dim))
    return level


def profile(number_of, total, limit, lean):
    weights = [(1 << 20) // math.isqrt(standing ** lean) + 1 for standing in range(2, number_of + 1)]
    rest, counts = total - limit - (number_of - 1), [1] * (number_of - 1)
    while rest > 0:
        free = [i for i in range(number_of - 1) if counts[i] < limit]
        whole, left = sum([weights[i] for i in free]), rest
        for i in free:
            extra = min(limit - counts[i], max(1, left * weights[i] // whole), rest)
            counts[i] = counts[i] + extra
            rest = rest - extra
    return np.array([limit] + counts)


def ragged(own_key, number_of, total, limit, slope):
    if number_of == 2:
        one = jax.random.randint(own_key, (), max(1, total - limit), min(limit, total - 1) + 1)
        return jnp.stack([one, total - one])
    sizes = jnp.asarray(profile(number_of, total, limit, slope), jnp.int32)
    couples = (number_of - 1) // 2
    donor, taker = sizes[1:1 + 2 * couples:2], sizes[2:2 + 2 * couples:2]
    slack = jnp.minimum(donor - 1, limit - taker)
    moved = jax.random.randint(jax.random.fold_in(own_key, 1), (couples,), 0, 1 << 20) % (slack + 1)
    sizes = sizes.at[1:1 + 2 * couples:2].set(donor - moved).at[2:2 + 2 * couples:2].set(taker + moved)
    return sizes[jax.random.permutation(jax.random.fold_in(own_key, 2), number_of)]


def scatter_about(stream_key, dims, spread, limit, cuts=(), held_as=jnp.bfloat16):
    values = jax.random.normal(stream_key, dims, jnp.float32) * spread
    if len(cuts) > 0:
        values = level_of(stream_key, dims, cuts, -0.22, 0.18) * values
    return jnp.clip(values, min=-limit, max=limit).astype(held_as)


def setup_inputs(seed: int = 0, part: int = 0) -> dict:
    seeds = jax.random.split(jax.random.key(seed), 8)
    own_keys = jax.random.split(jax.random.fold_in(seeds[7], part), 8)
    return {
        "q_latent": draw_q_latent(jax.random.fold_in(jax.random.fold_in(seeds[7], part), 71), part),
        "q_rope": draw_q_rope(jax.random.fold_in(jax.random.fold_in(seeds[7], part), 71), part),
        "latent_cache": draw_latent_cache(jax.random.fold_in(jax.random.fold_in(seeds[7], part), 71), part),
        "page_table": draw_page_table(jax.random.fold_in(jax.random.fold_in(seeds[7], part), 71), part),
        "lengths": ragged(own_keys[4], ROWS, ROWS * MAXP * PAGE * 5 // 8, MAXP * PAGE, 2).astype(jnp.int32),
        "w_uv": scatter_about(seeds[5], (H, C, V), (16.0 / C ** 0.5), 6.0, ((0, 8),)),
        "w_out": scatter_about(seeds[6], (H * V, D), (H * V) ** -0.5, 0.046875, ((0, 8),)),
    }


NEG = -1e30


def reference(q_latent, q_rope, latent_cache, page_table, lengths, w_uv, w_out):
    score_scale = (V + ROPE) ** -0.5
    query = jnp.concatenate([q_latent, q_rope], axis=2)
    position = jnp.arange(MAXP * PAGE, dtype=jnp.int32)

    def one_row(packed):
        row_query, row_pages, length = packed
        row_keys = latent_cache[row_pages].reshape(MAXP * PAGE, C + ROPE)
        scores = jnp.dot(row_query, row_keys.T, preferred_element_type=jnp.float32) * score_scale
        live_mask = (position < length)[None, :]
        scores = jnp.where(live_mask, scores, jnp.float32(NEG))
        top_score = jnp.max(scores, axis=1)
        weights = jnp.where(live_mask, jnp.exp(scores - top_score[:, None]), jnp.float32(0.0)).astype(jnp.bfloat16)
        row_total = jnp.sum(weights.astype(jnp.float32), axis=1)
        summed = jnp.dot(weights, row_keys[:, :C], preferred_element_type=jnp.float32)
        return (summed / row_total[:, None]).astype(jnp.bfloat16)

    attended = lax.map(one_row, (query, page_table, lengths))
    head_out = jnp.einsum("rhc,hcv->rhv", attended.astype(jnp.float32), w_uv.astype(jnp.float32)).astype(jnp.bfloat16)
    flat = head_out.reshape(ROWS, H * V)
    return jnp.dot(flat, w_out, preferred_element_type=jnp.float32).astype(jnp.bfloat16)
```

```python
import functools

import jax
import jax.numpy as jnp
from jax import lax
from jax.experimental import pallas as pl
from jax.experimental.pallas import tpu as pltpu
from jax.sharding import PartitionSpec as P

ROPE = 64
V = 128


NEG = -1e30
FLOOR = -1e29
N = 8
TILE = 1024
LANES = 128
GROUPS = ((0, 1), (2, 3), (4, 5), (6, 7))
SEND_ORDER = (6, 7, 2, 4, 3, 5, 1)


def finish(row_sums, row_outs, w_uv, w_out):
    latent = (row_outs / row_sums[..., None]).astype(jnp.bfloat16)
    head_out = jnp.einsum("rhc,hcv->rhv", latent, w_uv, preferred_element_type=jnp.float32).astype(
        jnp.bfloat16
    )
    flat = head_out.reshape(head_out.shape[0], -1)
    return jnp.dot(flat, w_out, preferred_element_type=jnp.float32)


def local(q_latent, q_rope, latent_cache, page_table, lengths, w_uv, w_out):
    score_scale = (V + ROPE) ** (-0.5)
    local_query = jnp.concatenate([q_latent, q_rope], axis=2)
    all_query = lax.all_gather(local_query, "ctx", axis=1, tiled=True)
    pages_here = latent_cache.shape[0]
    page_len = latent_cache.shape[1]
    row_count = page_table.shape[0]
    slot_width = page_table.shape[1]
    slot_count = row_count * slot_width
    latent_width = q_latent.shape[2]
    inverse = (
        jnp.zeros((slot_count,), jnp.int32)
        .at[page_table.reshape(-1)]
        .set(jnp.arange(slot_count, dtype=jnp.int32))
    )
    first_page = lax.axis_index("ctx") * pages_here
    slot_ids = lax.dynamic_slice_in_dim(inverse, first_page, pages_here)
    owner_row = slot_ids // slot_width
    logical = slot_ids % slot_width
    page_query = all_query[owner_row]
    scores = (
        jnp.einsum("phc,ptc->pht", page_query, latent_cache, preferred_element_type=jnp.float32)
        * score_scale
    )
    position = logical[:, None] * page_len + jnp.arange(page_len, dtype=jnp.int32)[None, :]
    live_mask = position < lengths[owner_row][:, None]
    scores = jnp.where(live_mask[:, None, :], scores, jnp.float32(NEG))
    page_top = jnp.max(scores, axis=2)
    member = owner_row[None, :] == jnp.arange(row_count, dtype=jnp.int32)[:, None]
    row_top = jnp.max(jnp.where(member[:, :, None], page_top[None, :, :], jnp.float32(NEG)), axis=1)
    row_shift = row_top[owner_row]
    weights = jnp.where(
        live_mask[:, None, :], jnp.exp(scores - row_shift[:, :, None]), jnp.float32(0.0)
    ).astype(jnp.bfloat16)
    page_sum = jnp.sum(weights.astype(jnp.float32), axis=2)
    page_out = jnp.einsum(
        "pht,ptc->phc",
        weights,
        latent_cache[:, :, :latent_width],
        preferred_element_type=jnp.float32,
    )
    onehot = member.astype(jnp.float32)
    row_sum = jnp.dot(onehot, page_sum, precision=lax.Precision.HIGHEST)
    row_out = jnp.dot(
        onehot, page_out.reshape(pages_here, -1), precision=lax.Precision.HIGHEST
    ).reshape(row_count, -1, latent_width)
    tops = lax.all_to_all(row_top[None], "ctx", split_axis=2, concat_axis=0, tiled=True)
    sums = lax.all_to_all(row_sum[None], "ctx", split_axis=2, concat_axis=0, tiled=True)
    outs = lax.all_to_all(
        row_out[None].astype(jnp.bfloat16), "ctx", split_axis=2, concat_axis=0, tiled=True
    ).astype(jnp.float32)
    best = jnp.max(tops, axis=0)
    factor = jnp.exp(tops - best[None])
    merged_sum = jnp.sum(factor * sums, axis=0)
    merged_out = jnp.sum(factor[..., None] * outs, axis=0)
    partial_out = finish(merged_sum, merged_out, w_uv, w_out)
    return lax.psum(partial_out, "ctx").astype(jnp.bfloat16)


def partner(me, k):
    peer = 0
    for bit in (1, 2, 4):
        mine = (me // bit) % 2
        peer = peer + bit * ((1 - mine) if k & bit else mine)
    return peer


def pieces(value, count):
    terms = []
    for _ in range(count):
        term = value.astype(jnp.bfloat16).astype(jnp.float32)
        terms.append(term)
        value = value - term
    return terms


def kernel(
    ql_ref, qr_ref, cache_ref, table_ref, len_ref, uv_ref, wo_ref, out_ref,
    qall, rope, kv, states, got, uv, wo, part, parts, flat, dense,
    local_sem, wo_sem, q_send, q_recv, s_send, s_recv, p_send, p_recv,
):
    rows, heads, width = ql_ref.shape
    pages, page_len, key_width = cache_ref.shape
    tokens = pages * page_len
    slots = table_ref.shape[1]
    tiles = wo.shape[0]
    scale = (V + ROPE) ** (-0.5)
    me = lax.axis_index("ctx")
    peers = [partner(me, k) for k in range(N)]

    barrier = pltpu.get_barrier_semaphore()
    for k in SEND_ORDER:
        pl.semaphore_signal(
            barrier, inc=1, device_id={"ctx": peers[k]}, device_id_type=pl.DeviceIdType.MESH
        )

    load_ql = pltpu.make_async_copy(ql_ref, qall.at[0, :, :, pl.ds(0, width)], local_sem.at[0])
    load_qr = pltpu.make_async_copy(qr_ref, rope, local_sem.at[1])
    load_kv = pltpu.make_async_copy(cache_ref, kv, local_sem.at[2])
    load_uv = pltpu.make_async_copy(uv_ref, uv, local_sem.at[3])
    load_ql.start()
    load_qr.start()
    load_kv.start()
    load_uv.start()

    def load_wo(j):
        return pltpu.make_async_copy(
            wo_ref.at[:, pl.ds(pl.multiple_of(j * TILE, TILE), TILE)], wo.at[j], wo_sem.at[j]
        )

    for j in range(tiles):
        load_wo(j).start()

    def remote(src, dst, send, recv, k):
        return pltpu.make_async_remote_copy(
            src_ref=src, dst_ref=dst, send_sem=send, recv_sem=recv,
            device_id={"ctx": peers[k]}, device_id_type=pl.DeviceIdType.MESH,
        )

    def query_copy(k):
        return remote(qall.at[0], qall.at[k], q_send.at[k], q_recv.at[k], k)

    def state_copy(k):
        return remote(states.at[k], got.at[k], s_send.at[k], s_recv.at[k], k)

    load_ql.wait()
    load_qr.wait()
    qall[0, :, :, width:] = jnp.concatenate([rope[...], jnp.zeros_like(rope)], axis=2)
    pl.semaphore_wait(barrier, N - 1)
    for k in SEND_ORDER:
        query_copy(k).start()

    lane = lax.broadcasted_iota(jnp.int32, (1, tokens), 1)
    page = lane // page_len + me * pages
    offset = lane % page_len
    live = []
    for r in range(rows):
        limit = jnp.zeros((1, tokens), jnp.int32)
        for j in range(slots):
            limit = jnp.where(page == table_ref[r, j], len_ref[r] - j * page_len, limit)
        live.append(offset < limit)

    load_kv.wait()
    keys = kv[...].reshape(tokens, key_width)
    block = rows * heads
    for group in GROUPS:
        for k in group:
            if k:
                query_copy(k).wait_recv()
        first, count = group[0], len(group)
        query = qall[first : first + count].reshape(count * block, width + LANES)[:, :key_width]
        scores = (
            lax.dot_general(
                query, keys, (((1,), (1,)), ((), ())), preferred_element_type=jnp.float32
            )
            * scale
        )
        scores = jnp.concatenate(
            [
                jnp.where(live[i % rows], scores[i * heads : (i + 1) * heads], jnp.float32(NEG))
                for i in range(count * rows)
            ],
            axis=0,
        )
        top = jnp.max(scores, axis=1, keepdims=True)
        weights = jnp.exp(scores - jnp.maximum(top, jnp.float32(FLOOR))).astype(jnp.bfloat16)
        total = jnp.sum(weights.astype(jnp.float32), axis=1, keepdims=True)
        summed = jnp.dot(weights, keys[:, :width], preferred_element_type=jnp.float32)
        states[first : first + count, :, :, :width] = summed.astype(jnp.bfloat16).reshape(
            count, rows, heads, width
        )
        place = lax.broadcasted_iota(jnp.int32, (count * block, LANES), 1)
        stats = jnp.zeros((count * block, LANES), jnp.float32)
        for i, term in enumerate(pieces(top, 3) + pieces(total, 3)):
            stats = jnp.where(place == i, term, stats)
        states[first : first + count, :, :, width:] = stats.astype(jnp.bfloat16).reshape(
            count, rows, heads, LANES
        )
        for k in group:
            if k:
                state_copy(k).start()

    place = lax.broadcasted_iota(jnp.int32, (block, LANES), 1)
    tops, sums = [], []
    for k in range(N):
        if k:
            state_copy(k).wait_recv()
        source = got.at[k] if k else states.at[0]
        stats = source[:, :, width:].reshape(block, LANES).astype(jnp.float32)
        tops.append(jnp.sum(jnp.where(place < 3, stats, 0.0), axis=1, keepdims=True))
        sums.append(
            jnp.sum(jnp.where((place >= 3) & (place < 6), stats, 0.0), axis=1, keepdims=True)
        )
    best = functools.reduce(jnp.maximum, tops)
    merged = jnp.zeros((block, width), jnp.float32)
    merged_sum = jnp.zeros((block, 1), jnp.float32)
    for k in range(N):
        source = got.at[k] if k else states.at[0]
        factor = jnp.exp(tops[k] - best)
        merged_sum = merged_sum + factor * sums[k]
        merged = merged + factor * source[:, :, :width].reshape(block, width).astype(jnp.float32)
    latent = (merged / merged_sum).astype(jnp.bfloat16)

    load_uv.wait()
    for h in range(0, heads, 2):
        pair = jnp.concatenate([uv[h], uv[h + 1]], axis=1)
        product = jnp.dot(latent, pair, preferred_element_type=jnp.float32)
        for r in range(rows):
            for i in range(2):
                row = r * heads + h + i
                flat[r : r + 1, (h + i) * V : (h + i + 1) * V] = product[
                    row : row + 1, i * V : (i + 1) * V
                ]
    head_out = flat[...].astype(jnp.bfloat16)

    def step(j, carry):
        load_wo(j).wait()
        term = jnp.dot(head_out, wo[j], preferred_element_type=jnp.float32)
        for c in range(TILE // LANES):
            dense[c * rows : (c + 1) * rows, :] = term[:, c * LANES : (c + 1) * LANES]
        part[j] = dense[...].astype(jnp.bfloat16)
        for k in SEND_ORDER:
            remote(part.at[j], parts.at[k, j], p_send.at[k], p_recv.at[k], k).start()
        return carry

    lax.fori_loop(0, tiles, step, 0)

    terms = []
    for k in range(N):
        if k:
            remote(part, parts.at[k], p_send.at[k], p_recv.at[k], k).wait_recv()
        terms.append((parts[k] if k else part[...]).astype(jnp.float32))
    while len(terms) > 1:
        terms = [terms[i] + terms[i + 1] for i in range(0, len(terms), 2)]
    total = terms[0]
    for j in range(tiles):
        for c in range(TILE // LANES):
            start = j * TILE + c * LANES
            out_ref[:, start : start + LANES] = total[j, c * rows : (c + 1) * rows, :]

    for k in SEND_ORDER:
        query_copy(k).wait_send()
        state_copy(k).wait_send()
        remote(part, parts.at[k], p_send.at[k], p_recv.at[k], k).wait_send()


def fused(q_latent, q_rope, latent_cache, page_table, lengths, w_uv, w_out):
    rows, heads, width = q_latent.shape
    depth, columns = w_out.shape
    tiles = columns // TILE
    dense_rows = TILE // LANES * rows
    bf16 = jnp.bfloat16
    any_space = pl.BlockSpec(memory_space=pl.ANY)
    smem = pl.BlockSpec(memory_space=pltpu.SMEM)
    out = pl.pallas_call(
        kernel,
        out_shape=jax.ShapeDtypeStruct((rows, columns), jnp.float32),
        in_specs=[any_space, any_space, any_space, smem, smem, any_space, any_space],
        out_specs=pl.BlockSpec(memory_space=pltpu.VMEM),
        scratch_shapes=[
            pltpu.VMEM((N, rows, heads, width + LANES), bf16),
            pltpu.VMEM(q_rope.shape, bf16),
            pltpu.VMEM(latent_cache.shape, bf16),
            pltpu.VMEM((N, rows, heads, width + LANES), bf16),
            pltpu.VMEM((N, rows, heads, width + LANES), bf16),
            pltpu.VMEM(w_uv.shape, bf16),
            pltpu.VMEM((tiles, depth, TILE), bf16),
            pltpu.VMEM((tiles, dense_rows, LANES), bf16),
            pltpu.VMEM((N, tiles, dense_rows, LANES), bf16),
            pltpu.VMEM((rows, depth), jnp.float32),
            pltpu.VMEM((dense_rows, LANES), jnp.float32),
            pltpu.SemaphoreType.DMA((4,)),
            pltpu.SemaphoreType.DMA((tiles,)),
            pltpu.SemaphoreType.DMA((N,)),
            pltpu.SemaphoreType.DMA((N,)),
            pltpu.SemaphoreType.DMA((N,)),
            pltpu.SemaphoreType.DMA((N,)),
            pltpu.SemaphoreType.DMA((N,)),
            pltpu.SemaphoreType.DMA((N,)),
        ],
        compiler_params=pltpu.CompilerParams(
            collective_id=0, has_side_effects=True, vmem_limit_bytes=56 * 1024 * 1024
        ),
        cost_estimate=pl.CostEstimate(
            flops=2 * rows * depth * columns, bytes_accessed=2 * depth * columns, transcendentals=0
        ),
    )(q_latent, q_rope, latent_cache, page_table, lengths, w_uv, w_out)
    return out.astype(bf16)


def solution(mesh):
    in_specs = (
        P("grp", "ctx", None),
        P("grp", "ctx", None),
        P(("grp", "ctx"), None, None),
        P("grp", None),
        P("grp"),
        P("ctx", None, None),
        P("ctx", None),
    )
    out_specs = P("grp", None)

    def program(q_latent, q_rope, latent_cache, page_table, lengths, w_uv, w_out):
        rows, heads, width = q_latent.shape
        suits = (
            mesh.shape["ctx"] == N
            and rows * (TILE // LANES) == 16
            and heads % 16 == 0
            and width % LANES == 0
            and w_uv.shape[2] == V
            and w_out.shape[1] % TILE == 0
            and w_out.size * 2 <= 32 * 1024 * 1024
            and latent_cache.size * 2 <= 2 * 1024 * 1024
        )
        body = fused if suits else local
        return body(q_latent, q_rope, latent_cache, page_table, lengths, w_uv, w_out)

    return jax.shard_map(program, mesh=mesh, in_specs=in_specs, out_specs=out_specs, check_vma=False)
```

```python
import functools

import jax
import jax.numpy as jnp
from jax import lax
from jax.experimental import pallas as pl
from jax.experimental.pallas import tpu as pltpu
from jax.sharding import PartitionSpec as P

ROPE = 64
V = 128


NEG = -1e30
FLOOR = -1e29
N = 8
TILE = 1024
LANES = 128
CHIPS = 4
GROUPS = ((0, 1), (2, 3))
CHIP_ORDER = (3, 1, 2)
SEND_ORDER = (6, 7, 2, 4, 3, 5, 1)


def finish(row_sums, row_outs, w_uv, w_out):
    latent = (row_outs / row_sums[..., None]).astype(jnp.bfloat16)
    head_out = jnp.einsum("rhc,hcv->rhv", latent, w_uv, preferred_element_type=jnp.float32).astype(
        jnp.bfloat16
    )
    flat = head_out.reshape(head_out.shape[0], -1)
    return jnp.dot(flat, w_out, preferred_element_type=jnp.float32)


def local(q_latent, q_rope, latent_cache, page_table, lengths, w_uv, w_out):
    score_scale = (V + ROPE) ** (-0.5)
    local_query = jnp.concatenate([q_latent, q_rope], axis=2)
    all_query = lax.all_gather(local_query, "ctx", axis=1, tiled=True)
    pages_here = latent_cache.shape[0]
    page_len = latent_cache.shape[1]
    row_count = page_table.shape[0]
    slot_width = page_table.shape[1]
    slot_count = row_count * slot_width
    latent_width = q_latent.shape[2]
    inverse = (
        jnp.zeros((slot_count,), jnp.int32)
        .at[page_table.reshape(-1)]
        .set(jnp.arange(slot_count, dtype=jnp.int32))
    )
    first_page = lax.axis_index("ctx") * pages_here
    slot_ids = lax.dynamic_slice_in_dim(inverse, first_page, pages_here)
    owner_row = slot_ids // slot_width
    logical = slot_ids % slot_width
    page_query = all_query[owner_row]
    scores = (
        jnp.einsum("phc,ptc->pht", page_query, latent_cache, preferred_element_type=jnp.float32)
        * score_scale
    )
    position = logical[:, None] * page_len + jnp.arange(page_len, dtype=jnp.int32)[None, :]
    live_mask = position < lengths[owner_row][:, None]
    scores = jnp.where(live_mask[:, None, :], scores, jnp.float32(NEG))
    page_top = jnp.max(scores, axis=2)
    member = owner_row[None, :] == jnp.arange(row_count, dtype=jnp.int32)[:, None]
    row_top = jnp.max(jnp.where(member[:, :, None], page_top[None, :, :], jnp.float32(NEG)), axis=1)
    row_shift = row_top[owner_row]
    weights = jnp.where(
        live_mask[:, None, :], jnp.exp(scores - row_shift[:, :, None]), jnp.float32(0.0)
    ).astype(jnp.bfloat16)
    page_sum = jnp.sum(weights.astype(jnp.float32), axis=2)
    page_out = jnp.einsum(
        "pht,ptc->phc",
        weights,
        latent_cache[:, :, :latent_width],
        preferred_element_type=jnp.float32,
    )
    onehot = member.astype(jnp.float32)
    row_sum = jnp.dot(onehot, page_sum, precision=lax.Precision.HIGHEST)
    row_out = jnp.dot(
        onehot, page_out.reshape(pages_here, -1), precision=lax.Precision.HIGHEST
    ).reshape(row_count, -1, latent_width)
    tops = lax.all_to_all(row_top[None], "ctx", split_axis=2, concat_axis=0, tiled=True)
    sums = lax.all_to_all(row_sum[None], "ctx", split_axis=2, concat_axis=0, tiled=True)
    outs = lax.all_to_all(
        row_out[None].astype(jnp.bfloat16), "ctx", split_axis=2, concat_axis=0, tiled=True
    ).astype(jnp.float32)
    best = jnp.max(tops, axis=0)
    factor = jnp.exp(tops - best[None])
    merged_sum = jnp.sum(factor * sums, axis=0)
    merged_out = jnp.sum(factor[..., None] * outs, axis=0)
    partial_out = finish(merged_sum, merged_out, w_uv, w_out)
    return lax.psum(partial_out, "ctx").astype(jnp.bfloat16)


def partner(me, k):
    peer = 0
    for bit in (1, 2, 4):
        mine = (me // bit) % 2
        peer = peer + bit * ((1 - mine) if k & bit else mine)
    return peer


def pieces(value, count):
    terms = []
    for _ in range(count):
        term = value.astype(jnp.bfloat16).astype(jnp.float32)
        terms.append(term)
        value = value - term
    return terms


def kernel(
    ql_ref, qr_ref, cache_ref, table_hbm, len_hbm, uv_ref, wo_ref, out_ref,
    qall, rope, kv, states, got, uv, wo, part, parts, flat, dense, table_ref, len_ref,
    local_sem, wo_sem, kv_send, kv_recv, q_send, q_recv, s_send, s_recv, p_send, p_recv,
):
    rows, heads, width = ql_ref.shape
    pages, page_len, key_width = cache_ref.shape
    tokens = 2 * pages * page_len
    slots = table_ref.shape[1]
    tiles = wo.shape[0]
    scale = (V + ROPE) ** (-0.5)
    me = lax.axis_index("ctx")
    peers = [partner(me, k) for k in range(N)]

    barrier = pltpu.get_barrier_semaphore()
    for k in SEND_ORDER:
        pl.semaphore_signal(
            barrier, inc=1, device_id={"ctx": peers[k]}, device_id_type=pl.DeviceIdType.MESH
        )

    load_ql = pltpu.make_async_copy(ql_ref, qall.at[0, :, :, pl.ds(0, width)], local_sem.at[0])
    load_qr = pltpu.make_async_copy(qr_ref, rope, local_sem.at[1])
    load_kv = pltpu.make_async_copy(cache_ref, kv.at[0], local_sem.at[2])
    load_uv = pltpu.make_async_copy(uv_ref, uv, local_sem.at[3])
    load_table = pltpu.make_async_copy(table_hbm, table_ref, local_sem.at[4])
    load_len = pltpu.make_async_copy(len_hbm, len_ref, local_sem.at[5])
    load_ql.start()
    load_qr.start()
    load_table.start()
    load_len.start()
    load_kv.start()
    load_uv.start()

    def load_wo(j):
        return pltpu.make_async_copy(
            wo_ref.at[:, pl.ds(pl.multiple_of(j * TILE, TILE), TILE)], wo.at[j], wo_sem.at[j]
        )

    for j in range(tiles):
        load_wo(j).start()

    def remote(src, dst, send, recv, k):
        return pltpu.make_async_remote_copy(
            src_ref=src, dst_ref=dst, send_sem=send, recv_sem=recv,
            device_id={"ctx": peers[k]}, device_id_type=pl.DeviceIdType.MESH,
        )

    def query_copy(e):
        return remote(qall.at[0], qall.at[e], q_send.at[e], q_recv.at[e], 2 * e)

    def state_copy(e):
        return remote(states.at[e], got.at[e], s_send.at[e], s_recv.at[e], 2 * e)

    swap = remote(cache_ref, kv.at[1], kv_send, kv_recv, 1)

    load_ql.wait()
    load_qr.wait()
    qall[0, :, :, width:] = jnp.concatenate([rope[...], jnp.zeros_like(rope)], axis=2)
    pl.semaphore_wait(barrier, N - 1)
    for e in CHIP_ORDER:
        query_copy(e).start()
    swap.start()

    load_table.wait()
    load_len.wait()
    lane = lax.broadcasted_iota(jnp.int32, (1, tokens), 1)
    page = lane // page_len
    page = jnp.where(page < pages, page + me * pages, page + (peers[1] - 1) * pages)
    offset = lane % page_len
    live = []
    for r in range(rows):
        limit = jnp.zeros((1, tokens), jnp.int32)
        for j in range(slots):
            limit = jnp.where(page == table_ref[r, j], len_ref[r] - j * page_len, limit)
        live.append(offset < limit)

    load_kv.wait()
    swap.wait_recv()
    keys = kv[...].reshape(tokens, key_width)
    block = rows * heads
    for group in GROUPS:
        for e in group:
            if e:
                query_copy(e).wait_recv()
        first, count = group[0], len(group)
        query = qall[first : first + count].reshape(count * block, width + LANES)[:, :key_width]
        scores = (
            lax.dot_general(
                query, keys, (((1,), (1,)), ((), ())), preferred_element_type=jnp.float32
            )
            * scale
        )
        scores = jnp.concatenate(
            [
                jnp.where(live[i % rows], scores[i * heads : (i + 1) * heads], jnp.float32(NEG))
                for i in range(count * rows)
            ],
            axis=0,
        )
        top = jnp.max(scores, axis=1, keepdims=True)
        weights = jnp.exp(scores - jnp.maximum(top, jnp.float32(FLOOR))).astype(jnp.bfloat16)
        total = jnp.sum(weights.astype(jnp.float32), axis=1, keepdims=True)
        summed = jnp.dot(weights, keys[:, :width], preferred_element_type=jnp.float32)
        states[first : first + count, :, :, :width] = summed.astype(jnp.bfloat16).reshape(
            count, rows, heads, width
        )
        place = lax.broadcasted_iota(jnp.int32, (count * block, LANES), 1)
        stats = jnp.zeros((count * block, LANES), jnp.float32)
        for i, term in enumerate(pieces(top, 3) + pieces(total, 3)):
            stats = jnp.where(place == i, term, stats)
        states[first : first + count, :, :, width:] = stats.astype(jnp.bfloat16).reshape(
            count, rows, heads, LANES
        )
        for e in group:
            if e:
                state_copy(e).start()

    place = lax.broadcasted_iota(jnp.int32, (block, LANES), 1)
    tops, sums = [], []
    for e in range(CHIPS):
        if e:
            state_copy(e).wait_recv()
        source = got.at[e] if e else states.at[0]
        stats = source[:, :, width:].reshape(block, LANES).astype(jnp.float32)
        tops.append(jnp.sum(jnp.where(place < 3, stats, 0.0), axis=1, keepdims=True))
        sums.append(
            jnp.sum(jnp.where((place >= 3) & (place < 6), stats, 0.0), axis=1, keepdims=True)
        )
    best = functools.reduce(jnp.maximum, tops)
    merged = jnp.zeros((block, width), jnp.float32)
    merged_sum = jnp.zeros((block, 1), jnp.float32)
    for e in range(CHIPS):
        source = got.at[e] if e else states.at[0]
        factor = jnp.exp(tops[e] - best)
        merged_sum = merged_sum + factor * sums[e]
        merged = merged + factor * source[:, :, :width].reshape(block, width).astype(jnp.float32)
    latent = (merged / merged_sum).astype(jnp.bfloat16)

    load_uv.wait()
    for h in range(0, heads, 2):
        pair = jnp.concatenate([uv[h], uv[h + 1]], axis=1)
        product = jnp.dot(latent, pair, preferred_element_type=jnp.float32)
        for r in range(rows):
            for i in range(2):
                row = r * heads + h + i
                flat[r : r + 1, (h + i) * V : (h + i + 1) * V] = product[
                    row : row + 1, i * V : (i + 1) * V
                ]
    head_out = flat[...].astype(jnp.bfloat16)

    def step(j, carry):
        load_wo(j).wait()
        term = jnp.dot(head_out, wo[j], preferred_element_type=jnp.float32)
        for c in range(TILE // LANES):
            dense[c * rows : (c + 1) * rows, :] = term[:, c * LANES : (c + 1) * LANES]
        part[j] = dense[...].astype(jnp.bfloat16)
        for k in SEND_ORDER:
            remote(part.at[j], parts.at[k, j], p_send.at[k], p_recv.at[k], k).start()
        return carry

    lax.fori_loop(0, tiles, step, 0)

    terms = []
    for k in range(N):
        if k:
            remote(part, parts.at[k], p_send.at[k], p_recv.at[k], k).wait_recv()
        terms.append((parts[k] if k else part[...]).astype(jnp.float32))
    while len(terms) > 1:
        terms = [terms[i] + terms[i + 1] for i in range(0, len(terms), 2)]
    total = terms[0]
    for j in range(tiles):
        for c in range(TILE // LANES):
            start = j * TILE + c * LANES
            out_ref[:, start : start + LANES] = total[j, c * rows : (c + 1) * rows, :]

    swap.wait_send()
    for e in CHIP_ORDER:
        query_copy(e).wait_send()
        state_copy(e).wait_send()
    for k in SEND_ORDER:
        remote(part, parts.at[k], p_send.at[k], p_recv.at[k], k).wait_send()


def fused(q_latent, q_rope, latent_cache, page_table, lengths, w_uv, w_out):
    rows, heads, width = q_latent.shape
    depth, columns = w_out.shape
    tiles = columns // TILE
    dense_rows = TILE // LANES * rows
    bf16 = jnp.bfloat16
    any_space = pl.BlockSpec(memory_space=pl.ANY)
    out = pl.pallas_call(
        kernel,
        out_shape=pltpu.VMEM((rows, columns), jnp.float32),
        in_specs=[any_space] * 7,
        out_specs=pl.BlockSpec(memory_space=pltpu.VMEM),
        scratch_shapes=[
            pltpu.VMEM((CHIPS, rows, heads, width + LANES), bf16),
            pltpu.VMEM(q_rope.shape, bf16),
            pltpu.VMEM((2,) + latent_cache.shape, bf16),
            pltpu.VMEM((CHIPS, rows, heads, width + LANES), bf16),
            pltpu.VMEM((CHIPS, rows, heads, width + LANES), bf16),
            pltpu.VMEM(w_uv.shape, bf16),
            pltpu.VMEM((tiles, depth, TILE), bf16),
            pltpu.VMEM((tiles, dense_rows, LANES), bf16),
            pltpu.VMEM((N, tiles, dense_rows, LANES), bf16),
            pltpu.VMEM((rows, depth), jnp.float32),
            pltpu.VMEM((dense_rows, LANES), jnp.float32),
            pltpu.SMEM(page_table.shape, jnp.int32),
            pltpu.SMEM(lengths.shape, jnp.int32),
            pltpu.SemaphoreType.DMA((6,)),
            pltpu.SemaphoreType.DMA((tiles,)),
            pltpu.SemaphoreType.DMA,
            pltpu.SemaphoreType.DMA,
            pltpu.SemaphoreType.DMA((CHIPS,)),
            pltpu.SemaphoreType.DMA((CHIPS,)),
            pltpu.SemaphoreType.DMA((CHIPS,)),
            pltpu.SemaphoreType.DMA((CHIPS,)),
            pltpu.SemaphoreType.DMA((N,)),
            pltpu.SemaphoreType.DMA((N,)),
        ],
        compiler_params=pltpu.CompilerParams(
            collective_id=0, has_side_effects=True, vmem_limit_bytes=56 * 1024 * 1024
        ),
        cost_estimate=pl.CostEstimate(
            flops=2 * rows * depth * columns, bytes_accessed=2 * depth * columns, transcendentals=0
        ),
    )(q_latent, q_rope, latent_cache, page_table, lengths, w_uv, w_out)
    return out.astype(bf16)


def solution(mesh):
    in_specs = (
        P("grp", "ctx", None),
        P("grp", "ctx", None),
        P(("grp", "ctx"), None, None),
        P("grp", None),
        P("grp"),
        P("ctx", None, None),
        P("ctx", None),
    )
    out_specs = P("grp", None)

    def program(q_latent, q_rope, latent_cache, page_table, lengths, w_uv, w_out):
        rows, heads, width = q_latent.shape
        suits = (
            mesh.shape["ctx"] == N
            and rows * (TILE // LANES) == 16
            and heads % 16 == 0
            and width % LANES == 0
            and w_uv.shape[2] == V
            and w_out.shape[1] % TILE == 0
            and w_out.size * 2 <= 32 * 1024 * 1024
            and latent_cache.size * 2 <= 2 * 1024 * 1024
        )
        body = fused if suits else local
        return body(q_latent, q_rope, latent_cache, page_table, lengths, w_uv, w_out)

    return jax.shard_map(program, mesh=mesh, in_specs=in_specs, out_specs=out_specs, check_vma=False)
```

```python
import functools

import jax
import jax.numpy as jnp
from jax import lax
from jax.experimental import pallas as pl
from jax.experimental.pallas import tpu as pltpu
from jax.sharding import PartitionSpec as P

ROPE = 64
V = 128


NEG = -1e30
FLOOR = -1e29
N = 8
SPAN = 256
LANES = 128
CHIPS = 4
GROUPS = ((0, 1), (2, 3))
CHIP_ORDER = (3, 1, 2)
ZS = 4


def finish(row_sums, row_outs, w_uv, w_out):
    latent = (row_outs / row_sums[..., None]).astype(jnp.bfloat16)
    head_out = jnp.einsum("rhc,hcv->rhv", latent, w_uv, preferred_element_type=jnp.float32).astype(
        jnp.bfloat16
    )
    flat = head_out.reshape(head_out.shape[0], -1)
    return jnp.dot(flat, w_out, preferred_element_type=jnp.float32)


def local(q_latent, q_rope, latent_cache, page_table, lengths, w_uv, w_out):
    score_scale = (V + ROPE) ** (-0.5)
    local_query = jnp.concatenate([q_latent, q_rope], axis=2)
    all_query = lax.all_gather(local_query, "ctx", axis=1, tiled=True)
    pages_here = latent_cache.shape[0]
    page_len = latent_cache.shape[1]
    row_count = page_table.shape[0]
    slot_width = page_table.shape[1]
    slot_count = row_count * slot_width
    latent_width = q_latent.shape[2]
    inverse = (
        jnp.zeros((slot_count,), jnp.int32)
        .at[page_table.reshape(-1)]
        .set(jnp.arange(slot_count, dtype=jnp.int32))
    )
    first_page = lax.axis_index("ctx") * pages_here
    slot_ids = lax.dynamic_slice_in_dim(inverse, first_page, pages_here)
    owner_row = slot_ids // slot_width
    logical = slot_ids % slot_width
    page_query = all_query[owner_row]
    scores = (
        jnp.einsum("phc,ptc->pht", page_query, latent_cache, preferred_element_type=jnp.float32)
        * score_scale
    )
    position = logical[:, None] * page_len + jnp.arange(page_len, dtype=jnp.int32)[None, :]
    live_mask = position < lengths[owner_row][:, None]
    scores = jnp.where(live_mask[:, None, :], scores, jnp.float32(NEG))
    page_top = jnp.max(scores, axis=2)
    member = owner_row[None, :] == jnp.arange(row_count, dtype=jnp.int32)[:, None]
    row_top = jnp.max(jnp.where(member[:, :, None], page_top[None, :, :], jnp.float32(NEG)), axis=1)
    row_shift = row_top[owner_row]
    weights = jnp.where(
        live_mask[:, None, :], jnp.exp(scores - row_shift[:, :, None]), jnp.float32(0.0)
    ).astype(jnp.bfloat16)
    page_sum = jnp.sum(weights.astype(jnp.float32), axis=2)
    page_out = jnp.einsum(
        "pht,ptc->phc",
        weights,
        latent_cache[:, :, :latent_width],
        preferred_element_type=jnp.float32,
    )
    onehot = member.astype(jnp.float32)
    row_sum = jnp.dot(onehot, page_sum, precision=lax.Precision.HIGHEST)
    row_out = jnp.dot(
        onehot, page_out.reshape(pages_here, -1), precision=lax.Precision.HIGHEST
    ).reshape(row_count, -1, latent_width)
    tops = lax.all_to_all(row_top[None], "ctx", split_axis=2, concat_axis=0, tiled=True)
    sums = lax.all_to_all(row_sum[None], "ctx", split_axis=2, concat_axis=0, tiled=True)
    outs = lax.all_to_all(
        row_out[None].astype(jnp.bfloat16), "ctx", split_axis=2, concat_axis=0, tiled=True
    ).astype(jnp.float32)
    best = jnp.max(tops, axis=0)
    factor = jnp.exp(tops - best[None])
    merged_sum = jnp.sum(factor * sums, axis=0)
    merged_out = jnp.sum(factor[..., None] * outs, axis=0)
    partial_out = finish(merged_sum, merged_out, w_uv, w_out)
    return lax.psum(partial_out, "ctx").astype(jnp.bfloat16)


def partner(me, k):
    peer = 0
    for bit in (1, 2, 4):
        mine = (me // bit) % 2
        peer = peer + bit * ((1 - mine) if k & bit else mine)
    return peer


def pieces(value, count):
    terms = []
    for _ in range(count):
        term = value.astype(jnp.bfloat16).astype(jnp.float32)
        terms.append(term)
        value = value - term
    return terms


def kernel(
    ql_ref, qr_ref, cache_ref, table_hbm, len_hbm, uv_ref, wo_ref, out_ref,
    qall, rope, kv, states, got, uv, wo, heads_out, spread, flat, part, parts, slices, final,
    table_ref, len_ref, local_sem, wo_sem, kv_send, kv_recv, q_send, q_recv, s_send, s_recv,
    h_send, h_recv, p_send, p_recv, f_send, f_recv,
):
    rows, heads, width = ql_ref.shape
    pages, page_len, key_width = cache_ref.shape
    tokens = 2 * pages * page_len
    slots = table_ref.shape[1]
    depth, share = wo.shape
    owners = share // SPAN
    scale = (V + ROPE) ** (-0.5)
    me = lax.axis_index("ctx")
    peers = [partner(me, k) for k in range(N)]

    zone = lax.axis_index("grp")
    others = [(k, dz) for dz in (2, 1, 3, 0) for k in (6, 7, 2, 4, 3, 5, 1, 0) if k or dz]

    def device(k, dz):
        return {"ctx": peers[k], "grp": lax.rem(zone + dz, ZS)}

    barrier = pltpu.get_barrier_semaphore()
    for k, dz in reversed(others):
        pl.semaphore_signal(
            barrier, inc=1, device_id=device(k, dz), device_id_type=pl.DeviceIdType.MESH
        )

    load_ql = pltpu.make_async_copy(ql_ref, qall.at[0, :, :, pl.ds(0, width)], local_sem.at[0])
    load_qr = pltpu.make_async_copy(qr_ref, rope, local_sem.at[1])
    load_kv = pltpu.make_async_copy(cache_ref, kv.at[0], local_sem.at[2])
    load_uv = pltpu.make_async_copy(uv_ref, uv, local_sem.at[3])
    load_table = pltpu.make_async_copy(table_hbm, table_ref, local_sem.at[4])
    load_len = pltpu.make_async_copy(len_hbm, len_ref, local_sem.at[5])
    load_ql.start()
    load_qr.start()
    load_table.start()
    load_len.start()
    load_kv.start()
    load_uv.start()

    def load_wo(j):
        band = pl.ds(j * (depth // 4), depth // 4)
        columns = pl.ds(pl.multiple_of(zone * share, SPAN), share)
        return pltpu.make_async_copy(wo_ref.at[band, columns], wo.at[band], wo_sem.at[j])

    for j in range(4):
        load_wo(j).start()

    def remote(src, dst, send, recv, k, dz=0):
        return pltpu.make_async_remote_copy(
            src_ref=src, dst_ref=dst, send_sem=send, recv_sem=recv,
            device_id=device(k, dz), device_id_type=pl.DeviceIdType.MESH,
        )

    def query_copy(e):
        return remote(qall.at[0], qall.at[e], q_send.at[e], q_recv.at[e], 2 * e)

    def state_copy(e):
        return remote(states.at[e], got.at[e], s_send.at[e], s_recv.at[e], 2 * e)

    swap = remote(cache_ref, kv.at[1], kv_send, kv_recv, 1)

    load_ql.wait()
    load_qr.wait()
    qall[0, :, :, width:] = jnp.concatenate([rope[...], jnp.zeros_like(rope)], axis=2)
    pl.semaphore_wait(barrier, N * ZS - 1)
    for e in CHIP_ORDER:
        query_copy(e).start()
    swap.start()

    load_table.wait()
    load_len.wait()
    lane = lax.broadcasted_iota(jnp.int32, (1, tokens), 1)
    page = lane // page_len
    page = jnp.where(page < pages, page + me * pages, page + (peers[1] - 1) * pages)
    offset = lane % page_len
    live = []
    for r in range(rows):
        limit = jnp.zeros((1, tokens), jnp.int32)
        for j in range(slots):
            limit = jnp.where(page == table_ref[r, j], len_ref[r] - j * page_len, limit)
        live.append(offset < limit)

    load_kv.wait()
    swap.wait_recv()
    keys = kv[...].reshape(tokens, key_width)
    block = rows * heads
    for group in GROUPS:
        for e in group:
            if e:
                query_copy(e).wait_recv()
        first, count = group[0], len(group)
        query = qall[first : first + count].reshape(count * block, width + LANES)[:, :key_width]
        scores = (
            lax.dot_general(
                query, keys, (((1,), (1,)), ((), ())), preferred_element_type=jnp.float32
            )
            * scale
        )
        scores = jnp.concatenate(
            [
                jnp.where(live[i % rows], scores[i * heads : (i + 1) * heads], jnp.float32(NEG))
                for i in range(count * rows)
            ],
            axis=0,
        )
        top = jnp.max(scores, axis=1, keepdims=True)
        weights = jnp.exp(scores - jnp.maximum(top, jnp.float32(FLOOR))).astype(jnp.bfloat16)
        total = jnp.sum(weights.astype(jnp.float32), axis=1, keepdims=True)
        summed = jnp.dot(weights, keys[:, :width], preferred_element_type=jnp.float32)
        states[first : first + count, :, :, :width] = summed.astype(jnp.bfloat16).reshape(
            count, rows, heads, width
        )
        place = lax.broadcasted_iota(jnp.int32, (count * block, LANES), 1)
        stats = jnp.zeros((count * block, LANES), jnp.float32)
        for i, term in enumerate(pieces(top, 3) + pieces(total, 3)):
            stats = jnp.where(place == i, term, stats)
        states[first : first + count, :, :, width:] = stats.astype(jnp.bfloat16).reshape(
            count, rows, heads, LANES
        )
        for e in group:
            if e:
                state_copy(e).start()

    place = lax.broadcasted_iota(jnp.int32, (block, LANES), 1)
    tops, sums = [], []
    for e in range(CHIPS):
        if e:
            state_copy(e).wait_recv()
        source = got.at[e] if e else states.at[0]
        stats = source[:, :, width:].reshape(block, LANES).astype(jnp.float32)
        tops.append(jnp.sum(jnp.where(place < 3, stats, 0.0), axis=1, keepdims=True))
        sums.append(
            jnp.sum(jnp.where((place >= 3) & (place < 6), stats, 0.0), axis=1, keepdims=True)
        )
    best = functools.reduce(jnp.maximum, tops)
    merged = jnp.zeros((block, width), jnp.float32)
    merged_sum = jnp.zeros((block, 1), jnp.float32)
    for e in range(CHIPS):
        source = got.at[e] if e else states.at[0]
        factor = jnp.exp(tops[e] - best)
        merged_sum = merged_sum + factor * sums[e]
        merged = merged + factor * source[:, :, :width].reshape(block, width).astype(jnp.float32)
    latent = (merged / merged_sum).astype(jnp.bfloat16)

    load_uv.wait()
    for h in range(0, heads, 2):
        pair = jnp.concatenate([uv[h], uv[h + 1]], axis=1)
        product = jnp.dot(latent, pair, preferred_element_type=jnp.float32)
        for r in range(rows):
            for i in range(2):
                row = r * heads + h + i
                spread[row : row + 1, :] = product[row : row + 1, i * V : (i + 1) * V]

    def head_copy(dz):
        back = (ZS - dz) % ZS
        return remote(heads_out.at[0], heads_out.at[back], h_send.at[dz], h_recv.at[back], 0, dz)

    def head_arrived(slot):
        return remote(heads_out.at[0], heads_out.at[slot], h_send.at[0], h_recv.at[slot], 0, slot)

    heads_out[0] = spread[0:block, :].astype(jnp.bfloat16)
    for dz in (2, 1, 3):
        head_copy(dz).start()
    for dz in (1, 3, 2):
        head_arrived(dz).wait_recv()
    for dz in range(ZS):
        spread[dz * block : (dz + 1) * block, :] = heads_out[dz].astype(jnp.float32)
    for h in range(heads):
        flat[:, h * V : (h + 1) * V] = spread[pl.ds(h, ZS * rows, stride=heads), :]
    head_out = flat[...].astype(jnp.bfloat16)

    for j in range(4):
        load_wo(j).wait()

    def part_copy(o):
        return pltpu.make_async_remote_copy(
            src_ref=part.at[o], dst_ref=parts.at[me], send_sem=p_send.at[o], recv_sem=p_recv,
            device_id={"ctx": o}, device_id_type=pl.DeviceIdType.MESH,
        )

    for o in range(owners):
        term = jnp.dot(
            head_out, wo[:, o * SPAN : (o + 1) * SPAN], preferred_element_type=jnp.float32
        )
        part[o] = jnp.concatenate([term[:, :LANES], term[:, LANES:]], axis=0).astype(jnp.bfloat16)

        @pl.when(me != o)
        def _():
            part_copy(o).start()

        @pl.when(me == o)
        def _():
            parts[o] = part[o]

    place = zone * N + me

    @pl.when(me < owners)
    def _():
        pltpu.make_async_copy(parts.at[pl.ds(0, N - 1)], parts.at[pl.ds(0, N - 1)], p_recv).wait()
        terms = [parts[c].astype(jnp.float32) for c in range(N)]
        while len(terms) > 1:
            terms = [terms[i] + terms[i + 1] for i in range(0, len(terms), 2)]
        total = terms[0]
        half = ZS * rows
        for dz in range(ZS):
            slices[dz] = jnp.concatenate(
                [total[i * half + dz * rows : i * half + (dz + 1) * rows] for i in range(2)], axis=0
            ).astype(jnp.bfloat16)
        for k, dz in others:
            remote(slices.at[dz], final.at[place], f_send, f_recv, k, dz).start()
        final[place] = slices[0]

    def arrived(count):
        some = final.at[pl.ds(0, count)]
        pltpu.make_async_copy(some, some, f_recv).wait()

    @pl.when(me < owners)
    def _():
        arrived(ZS * owners - 1)

    @pl.when(me >= owners)
    def _():
        arrived(ZS * owners)

    for z in range(ZS):
        for o in range(owners):
            block_out = final[z * N + o].astype(jnp.float32)
            for i in range(2):
                start = z * share + o * SPAN + i * LANES
                out_ref[:, start : start + LANES] = block_out[i * rows : (i + 1) * rows, :]

    swap.wait_send()
    for e in CHIP_ORDER:
        query_copy(e).wait_send()
        state_copy(e).wait_send()
    for dz in (1, 2, 3):
        head_copy(dz).wait_send()
    for o in range(owners):

        @pl.when(me != o)
        def _():
            part_copy(o).wait_send()

    @pl.when(me < owners)
    def _():
        sent = final.at[pl.ds(0, N * ZS - 1)]
        pltpu.make_async_copy(sent, sent, f_send).wait()


def fused(q_latent, q_rope, latent_cache, page_table, lengths, w_uv, w_out):
    rows, heads, width = q_latent.shape
    depth, columns = w_out.shape
    share = columns // ZS
    owners = share // SPAN
    block = rows * heads
    bf16 = jnp.bfloat16
    any_space = pl.BlockSpec(memory_space=pl.ANY)
    out = pl.pallas_call(
        kernel,
        out_shape=pltpu.VMEM((rows, columns), jnp.float32),
        in_specs=[any_space] * 7,
        out_specs=pl.BlockSpec(memory_space=pltpu.VMEM),
        scratch_shapes=[
            pltpu.VMEM((CHIPS, rows, heads, width + LANES), bf16),
            pltpu.VMEM(q_rope.shape, bf16),
            pltpu.VMEM((2,) + latent_cache.shape, bf16),
            pltpu.VMEM((CHIPS, rows, heads, width + LANES), bf16),
            pltpu.VMEM((CHIPS, rows, heads, width + LANES), bf16),
            pltpu.VMEM(w_uv.shape, bf16),
            pltpu.VMEM((depth, share), bf16),
            pltpu.VMEM((ZS, block, V), bf16),
            pltpu.VMEM((ZS * block, V), jnp.float32),
            pltpu.VMEM((ZS * rows, depth), jnp.float32),
            pltpu.VMEM((owners, 2 * ZS * rows, LANES), bf16),
            pltpu.VMEM((N, 2 * ZS * rows, LANES), bf16),
            pltpu.VMEM((ZS, 2 * rows, LANES), bf16),
            pltpu.VMEM((N * ZS, 2 * rows, LANES), bf16),
            pltpu.SMEM(page_table.shape, jnp.int32),
            pltpu.SMEM(lengths.shape, jnp.int32),
            pltpu.SemaphoreType.DMA((6,)),
            pltpu.SemaphoreType.DMA((4,)),
            pltpu.SemaphoreType.DMA,
            pltpu.SemaphoreType.DMA,
            pltpu.SemaphoreType.DMA((CHIPS,)),
            pltpu.SemaphoreType.DMA((CHIPS,)),
            pltpu.SemaphoreType.DMA((CHIPS,)),
            pltpu.SemaphoreType.DMA((CHIPS,)),
            pltpu.SemaphoreType.DMA((ZS,)),
            pltpu.SemaphoreType.DMA((ZS,)),
            pltpu.SemaphoreType.DMA((N,)),
            pltpu.SemaphoreType.DMA,
            pltpu.SemaphoreType.DMA,
            pltpu.SemaphoreType.DMA,
        ],
        compiler_params=pltpu.CompilerParams(
            collective_id=0, has_side_effects=True, vmem_limit_bytes=56 * 1024 * 1024
        ),
        cost_estimate=pl.CostEstimate(
            flops=2 * rows * depth * columns, bytes_accessed=2 * depth * share, transcendentals=0
        ),
    )(q_latent, q_rope, latent_cache, page_table, lengths, w_uv, w_out)
    return out.astype(bf16)


def solution(mesh):
    in_specs = (
        P("grp", "ctx", None),
        P("grp", "ctx", None),
        P(("grp", "ctx"), None, None),
        P("grp", None),
        P("grp"),
        P("ctx", None, None),
        P("ctx", None),
    )
    out_specs = P("grp", None)

    def program(q_latent, q_rope, latent_cache, page_table, lengths, w_uv, w_out):
        rows, heads, width = q_latent.shape
        suits = (
            mesh.shape["ctx"] == N
            and mesh.shape["grp"] == ZS
            and rows * ZS == 8
            and heads % 16 == 0
            and width % LANES == 0
            and w_uv.shape[2] == V
            and w_out.shape[1] % (ZS * SPAN) == 0
            and w_out.shape[1] <= N * ZS * SPAN
            and w_out.size * 2 <= 32 * 1024 * 1024
            and latent_cache.size * 2 <= 2 * 1024 * 1024
        )
        body = fused if suits else local
        return body(q_latent, q_rope, latent_cache, page_table, lengths, w_uv, w_out)

    return jax.shard_map(program, mesh=mesh, in_specs=in_specs, out_specs=out_specs, check_vma=False)
```

```python
import functools

import jax
import jax.numpy as jnp
from jax import lax
from jax.experimental import pallas as pl
from jax.experimental.pallas import tpu as pltpu
from jax.sharding import PartitionSpec as P

ROPE = 64
V = 128


NEG = -1e30
FLOOR = -1e29
N = 8
TILE = 1024
LANES = 128
CHIPS = 4
GROUPS = ((1, 2, 3), (0,))
EARLY = 1
LATE = 2
CHIP_ORDER = (3, 1, 2)
SEND_ORDER = (6, 7, 2, 4, 3, 5, 1)


def finish(row_sums, row_outs, w_uv, w_out):
    latent = (row_outs / row_sums[..., None]).astype(jnp.bfloat16)
    head_out = jnp.einsum("rhc,hcv->rhv", latent, w_uv, preferred_element_type=jnp.float32).astype(
        jnp.bfloat16
    )
    flat = head_out.reshape(head_out.shape[0], -1)
    return jnp.dot(flat, w_out, preferred_element_type=jnp.float32)


def local(q_latent, q_rope, latent_cache, page_table, lengths, w_uv, w_out):
    score_scale = (V + ROPE) ** (-0.5)
    local_query = jnp.concatenate([q_latent, q_rope], axis=2)
    all_query = lax.all_gather(local_query, "ctx", axis=1, tiled=True)
    pages_here = latent_cache.shape[0]
    page_len = latent_cache.shape[1]
    row_count = page_table.shape[0]
    slot_width = page_table.shape[1]
    slot_count = row_count * slot_width
    latent_width = q_latent.shape[2]
    inverse = (
        jnp.zeros((slot_count,), jnp.int32)
        .at[page_table.reshape(-1)]
        .set(jnp.arange(slot_count, dtype=jnp.int32))
    )
    first_page = lax.axis_index("ctx") * pages_here
    slot_ids = lax.dynamic_slice_in_dim(inverse, first_page, pages_here)
    owner_row = slot_ids // slot_width
    logical = slot_ids % slot_width
    page_query = all_query[owner_row]
    scores = (
        jnp.einsum("phc,ptc->pht", page_query, latent_cache, preferred_element_type=jnp.float32)
        * score_scale
    )
    position = logical[:, None] * page_len + jnp.arange(page_len, dtype=jnp.int32)[None, :]
    live_mask = position < lengths[owner_row][:, None]
    scores = jnp.where(live_mask[:, None, :], scores, jnp.float32(NEG))
    page_top = jnp.max(scores, axis=2)
    member = owner_row[None, :] == jnp.arange(row_count, dtype=jnp.int32)[:, None]
    row_top = jnp.max(jnp.where(member[:, :, None], page_top[None, :, :], jnp.float32(NEG)), axis=1)
    row_shift = row_top[owner_row]
    weights = jnp.where(
        live_mask[:, None, :], jnp.exp(scores - row_shift[:, :, None]), jnp.float32(0.0)
    ).astype(jnp.bfloat16)
    page_sum = jnp.sum(weights.astype(jnp.float32), axis=2)
    page_out = jnp.einsum(
        "pht,ptc->phc",
        weights,
        latent_cache[:, :, :latent_width],
        preferred_element_type=jnp.float32,
    )
    onehot = member.astype(jnp.float32)
    row_sum = jnp.dot(onehot, page_sum, precision=lax.Precision.HIGHEST)
    row_out = jnp.dot(
        onehot, page_out.reshape(pages_here, -1), precision=lax.Precision.HIGHEST
    ).reshape(row_count, -1, latent_width)
    tops = lax.all_to_all(row_top[None], "ctx", split_axis=2, concat_axis=0, tiled=True)
    sums = lax.all_to_all(row_sum[None], "ctx", split_axis=2, concat_axis=0, tiled=True)
    outs = lax.all_to_all(
        row_out[None].astype(jnp.bfloat16), "ctx", split_axis=2, concat_axis=0, tiled=True
    ).astype(jnp.float32)
    best = jnp.max(tops, axis=0)
    factor = jnp.exp(tops - best[None])
    merged_sum = jnp.sum(factor * sums, axis=0)
    merged_out = jnp.sum(factor[..., None] * outs, axis=0)
    partial_out = finish(merged_sum, merged_out, w_uv, w_out)
    return lax.psum(partial_out, "ctx").astype(jnp.bfloat16)


def partner(me, k):
    peer = 0
    for bit in (1, 2, 4):
        mine = (me // bit) % 2
        peer = peer + bit * ((1 - mine) if k & bit else mine)
    return peer


def pieces(value, count):
    terms = []
    for _ in range(count):
        term = value.astype(jnp.bfloat16).astype(jnp.float32)
        terms.append(term)
        value = value - term
    return terms


def kernel(
    ql_ref, qr_ref, cache_ref, table_hbm, len_hbm, uv_ref, wo_ref, out_ref,
    qall, rope, kv, states, got, uv, wo, part, parts, flat, dense, table_ref, len_ref,
    local_sem, wo_sem, kv_send, kv_recv, q_send, q_recv, s_send, s_recv, p_send, p_recv,
):
    rows, heads, width = ql_ref.shape
    pages, page_len, key_width = cache_ref.shape
    tokens = 2 * pages * page_len
    slots = table_ref.shape[1]
    tiles = wo.shape[0]
    scale = (V + ROPE) ** (-0.5)
    me = lax.axis_index("ctx")
    peers = [partner(me, k) for k in range(N)]

    barrier = pltpu.get_barrier_semaphore()
    for k in SEND_ORDER:
        pl.semaphore_signal(
            barrier, inc=1, device_id={"ctx": peers[k]}, device_id_type=pl.DeviceIdType.MESH
        )

    load_ql = pltpu.make_async_copy(ql_ref, qall.at[0, :, :, pl.ds(0, width)], local_sem.at[0])
    load_qr = pltpu.make_async_copy(qr_ref, rope, local_sem.at[1])
    load_kv = pltpu.make_async_copy(cache_ref, kv.at[0], local_sem.at[2])
    load_uv = pltpu.make_async_copy(uv_ref, uv, local_sem.at[3])
    load_table = pltpu.make_async_copy(table_hbm, table_ref, local_sem.at[4])
    load_len = pltpu.make_async_copy(len_hbm, len_ref, local_sem.at[5])
    load_ql.start()
    load_qr.start()
    load_table.start()
    load_len.start()
    load_kv.start()

    def load_wo(j):
        return pltpu.make_async_copy(
            wo_ref.at[:, pl.ds(pl.multiple_of(j * TILE, TILE), TILE)], wo.at[j], wo_sem.at[j]
        )

    for j in range(EARLY):
        load_wo(j).start()

    def remote(src, dst, send, recv, k):
        return pltpu.make_async_remote_copy(
            src_ref=src, dst_ref=dst, send_sem=send, recv_sem=recv,
            device_id={"ctx": peers[k]}, device_id_type=pl.DeviceIdType.MESH,
        )

    def query_copy(e):
        return remote(qall.at[0], qall.at[e], q_send.at[e], q_recv.at[e], 2 * e)

    def state_copy(e):
        return remote(states.at[e], got.at[e], s_send.at[e], s_recv.at[e], 2 * e)

    swap = remote(kv.at[0], kv.at[1], kv_send, kv_recv, 1)

    load_ql.wait()
    load_qr.wait()
    qall[0, :, :, width:] = jnp.concatenate([rope[...], jnp.zeros_like(rope)], axis=2)
    load_kv.wait()
    pl.semaphore_wait(barrier, N - 1)
    swap.start()
    for e in CHIP_ORDER:
        query_copy(e).start()
    load_uv.start()
    for j in range(EARLY, tiles):
        load_wo(j).start()

    load_table.wait()
    load_len.wait()
    lane = lax.broadcasted_iota(jnp.int32, (1, tokens), 1)
    page = lane // page_len
    page = jnp.where(page < pages, page + me * pages, page + (peers[1] - 1) * pages)
    offset = lane % page_len
    live = []
    for r in range(rows):
        limit = jnp.zeros((1, tokens), jnp.int32)
        for j in range(slots):
            limit = jnp.where(page == table_ref[r, j], len_ref[r] - j * page_len, limit)
        live.append(offset < limit)

    swap.wait_recv()
    keys = kv[...].reshape(tokens, key_width)
    block = rows * heads
    for group in GROUPS:
        for e in group:
            if e:
                query_copy(e).wait_recv()
        first, count = group[0], len(group)
        query = qall[first : first + count].reshape(count * block, width + LANES)[:, :key_width]
        scores = (
            lax.dot_general(
                query, keys, (((1,), (1,)), ((), ())), preferred_element_type=jnp.float32
            )
            * scale
        )
        scores = jnp.concatenate(
            [
                jnp.where(live[i % rows], scores[i * heads : (i + 1) * heads], jnp.float32(NEG))
                for i in range(count * rows)
            ],
            axis=0,
        )
        top = jnp.max(scores, axis=1, keepdims=True)
        weights = jnp.exp(scores - jnp.maximum(top, jnp.float32(FLOOR))).astype(jnp.bfloat16)
        total = jnp.sum(weights.astype(jnp.float32), axis=1, keepdims=True)
        summed = jnp.dot(weights, keys[:, :width], preferred_element_type=jnp.float32)
        states[first : first + count, :, :, :width] = summed.astype(jnp.bfloat16).reshape(
            count, rows, heads, width
        )
        place = lax.broadcasted_iota(jnp.int32, (count * block, LANES), 1)
        stats = jnp.zeros((count * block, LANES), jnp.float32)
        for i, term in enumerate(pieces(top, 3) + pieces(total, 3)):
            stats = jnp.where(place == i, term, stats)
        states[first : first + count, :, :, width:] = stats.astype(jnp.bfloat16).reshape(
            count, rows, heads, LANES
        )
        for e in group:
            if e:
                state_copy(e).start()

    place = lax.broadcasted_iota(jnp.int32, (block, LANES), 1)
    tops, sums = [], []
    for e in range(CHIPS):
        if e:
            state_copy(e).wait_recv()
        source = got.at[e] if e else states.at[0]
        stats = source[:, :, width:].reshape(block, LANES).astype(jnp.float32)
        tops.append(jnp.sum(jnp.where(place < 3, stats, 0.0), axis=1, keepdims=True))
        sums.append(
            jnp.sum(jnp.where((place >= 3) & (place < 6), stats, 0.0), axis=1, keepdims=True)
        )
    best = functools.reduce(jnp.maximum, tops)
    merged = jnp.zeros((block, width), jnp.float32)
    merged_sum = jnp.zeros((block, 1), jnp.float32)
    for e in range(CHIPS):
        source = got.at[e] if e else states.at[0]
        factor = jnp.exp(tops[e] - best)
        merged_sum = merged_sum + factor * sums[e]
        merged = merged + factor * source[:, :, :width].reshape(block, width).astype(jnp.float32)
    latent = (merged / merged_sum).astype(jnp.bfloat16)

    load_uv.wait()
    for h in range(0, heads, 2):
        pair = jnp.concatenate([uv[h], uv[h + 1]], axis=1)
        product = jnp.dot(latent, pair, preferred_element_type=jnp.float32)
        for r in range(rows):
            for i in range(2):
                row = r * heads + h + i
                flat[r : r + 1, (h + i) * V : (h + i + 1) * V] = product[
                    row : row + 1, i * V : (i + 1) * V
                ]
    head_out = flat[...].astype(jnp.bfloat16)

    def step(j, carry):
        load_wo(j).wait()
        term = jnp.dot(head_out, wo[j], preferred_element_type=jnp.float32)
        for c in range(TILE // LANES):
            dense[c * rows : (c + 1) * rows, :] = term[:, c * LANES : (c + 1) * LANES]
        part[j] = dense[...].astype(jnp.bfloat16)
        return carry

    for begin, end in ((0, tiles - LATE), (tiles - LATE, tiles)):
        lax.fori_loop(begin, end, step, 0)
        some = pl.ds(begin, end - begin)
        for k in SEND_ORDER:
            remote(part.at[some], parts.at[k, some], p_send.at[k], p_recv.at[k], k).start()

    terms = []
    for k in range(N):
        if k:
            remote(part, parts.at[k], p_send.at[k], p_recv.at[k], k).wait_recv()
        terms.append((parts[k] if k else part[...]).astype(jnp.float32))
    while len(terms) > 1:
        terms = [terms[i] + terms[i + 1] for i in range(0, len(terms), 2)]
    total = terms[0]
    for j in range(tiles):
        for c in range(TILE // LANES):
            start = j * TILE + c * LANES
            out_ref[:, start : start + LANES] = total[j, c * rows : (c + 1) * rows, :]

    swap.wait_send()
    for e in CHIP_ORDER:
        query_copy(e).wait_send()
        state_copy(e).wait_send()
    for k in SEND_ORDER:
        remote(part, parts.at[k], p_send.at[k], p_recv.at[k], k).wait_send()


def fused(q_latent, q_rope, latent_cache, page_table, lengths, w_uv, w_out):
    rows, heads, width = q_latent.shape
    depth, columns = w_out.shape
    tiles = columns // TILE
    dense_rows = TILE // LANES * rows
    bf16 = jnp.bfloat16
    any_space = pl.BlockSpec(memory_space=pl.ANY)
    out = pl.pallas_call(
        kernel,
        out_shape=pltpu.VMEM((rows, columns), jnp.float32),
        in_specs=[any_space] * 7,
        out_specs=pl.BlockSpec(memory_space=pltpu.VMEM),
        scratch_shapes=[
            pltpu.VMEM((CHIPS, rows, heads, width + LANES), bf16),
            pltpu.VMEM(q_rope.shape, bf16),
            pltpu.VMEM((2,) + latent_cache.shape, bf16),
            pltpu.VMEM((CHIPS, rows, heads, width + LANES), bf16),
            pltpu.VMEM((CHIPS, rows, heads, width + LANES), bf16),
            pltpu.VMEM(w_uv.shape, bf16),
            pltpu.VMEM((tiles, depth, TILE), bf16),
            pltpu.VMEM((tiles, dense_rows, LANES), bf16),
            pltpu.VMEM((N, tiles, dense_rows, LANES), bf16),
            pltpu.VMEM((rows, depth), jnp.float32),
            pltpu.VMEM((dense_rows, LANES), jnp.float32),
            pltpu.SMEM(page_table.shape, jnp.int32),
            pltpu.SMEM(lengths.shape, jnp.int32),
            pltpu.SemaphoreType.DMA((6,)),
            pltpu.SemaphoreType.DMA((tiles,)),
            pltpu.SemaphoreType.DMA,
            pltpu.SemaphoreType.DMA,
            pltpu.SemaphoreType.DMA((CHIPS,)),
            pltpu.SemaphoreType.DMA((CHIPS,)),
            pltpu.SemaphoreType.DMA((CHIPS,)),
            pltpu.SemaphoreType.DMA((CHIPS,)),
            pltpu.SemaphoreType.DMA((N,)),
            pltpu.SemaphoreType.DMA((N,)),
        ],
        compiler_params=pltpu.CompilerParams(
            collective_id=0, has_side_effects=True, vmem_limit_bytes=56 * 1024 * 1024
        ),
        cost_estimate=pl.CostEstimate(
            flops=2 * rows * depth * columns, bytes_accessed=2 * depth * columns, transcendentals=0
        ),
    )(q_latent, q_rope, latent_cache, page_table, lengths, w_uv, w_out)
    return out.astype(bf16)


def solution(mesh):
    in_specs = (
        P("grp", "ctx", None),
        P("grp", "ctx", None),
        P(("grp", "ctx"), None, None),
        P("grp", None),
        P("grp"),
        P("ctx", None, None),
        P("ctx", None),
    )
    out_specs = P("grp", None)

    def program(q_latent, q_rope, latent_cache, page_table, lengths, w_uv, w_out):
        rows, heads, width = q_latent.shape
        suits = (
            mesh.shape["ctx"] == N
            and rows * (TILE // LANES) == 16
            and heads % 16 == 0
            and width % LANES == 0
            and w_uv.shape[2] == V
            and w_out.shape[1] % TILE == 0
            and w_out.shape[1] > LATE * TILE
            and w_out.size * 2 <= 32 * 1024 * 1024
            and latent_cache.size * 2 <= 2 * 1024 * 1024
        )
        body = fused if suits else local
        return body(q_latent, q_rope, latent_cache, page_table, lengths, w_uv, w_out)

    return jax.shard_map(program, mesh=mesh, in_specs=in_specs, out_specs=out_specs, check_vma=False)
```

```python
import functools

import jax
import jax.numpy as jnp
from jax import lax
from jax.experimental import pallas as pl
from jax.experimental.pallas import tpu as pltpu
from jax.sharding import PartitionSpec as P

ROPE = 64
V = 128


NEG = -1e30
FLOOR = -1e29
N = 8
TILE = 1024
LANES = 128
CHIPS = 4
GROUPS = ((1, 2, 3), (0,))
EARLY = 3
LATE = 2
CHIP_ORDER = (3, 1, 2)
SEND_ORDER = (6, 7, 2, 4, 3, 5, 1)


def finish(row_sums, row_outs, w_uv, w_out):
    latent = (row_outs / row_sums[..., None]).astype(jnp.bfloat16)
    head_out = jnp.einsum("rhc,hcv->rhv", latent, w_uv, preferred_element_type=jnp.float32).astype(
        jnp.bfloat16
    )
    flat = head_out.reshape(head_out.shape[0], -1)
    return jnp.dot(flat, w_out, preferred_element_type=jnp.float32)


def local(q_latent, q_rope, latent_cache, page_table, lengths, w_uv, w_out):
    score_scale = (V + ROPE) ** (-0.5)
    local_query = jnp.concatenate([q_latent, q_rope], axis=2)
    all_query = lax.all_gather(local_query, "ctx", axis=1, tiled=True)
    pages_here = latent_cache.shape[0]
    page_len = latent_cache.shape[1]
    row_count = page_table.shape[0]
    slot_width = page_table.shape[1]
    slot_count = row_count * slot_width
    latent_width = q_latent.shape[2]
    inverse = (
        jnp.zeros((slot_count,), jnp.int32)
        .at[page_table.reshape(-1)]
        .set(jnp.arange(slot_count, dtype=jnp.int32))
    )
    first_page = lax.axis_index("ctx") * pages_here
    slot_ids = lax.dynamic_slice_in_dim(inverse, first_page, pages_here)
    owner_row = slot_ids // slot_width
    logical = slot_ids % slot_width
    page_query = all_query[owner_row]
    scores = (
        jnp.einsum("phc,ptc->pht", page_query, latent_cache, preferred_element_type=jnp.float32)
        * score_scale
    )
    position = logical[:, None] * page_len + jnp.arange(page_len, dtype=jnp.int32)[None, :]
    live_mask = position < lengths[owner_row][:, None]
    scores = jnp.where(live_mask[:, None, :], scores, jnp.float32(NEG))
    page_top = jnp.max(scores, axis=2)
    member = owner_row[None, :] == jnp.arange(row_count, dtype=jnp.int32)[:, None]
    row_top = jnp.max(jnp.where(member[:, :, None], page_top[None, :, :], jnp.float32(NEG)), axis=1)
    row_shift = row_top[owner_row]
    weights = jnp.where(
        live_mask[:, None, :], jnp.exp(scores - row_shift[:, :, None]), jnp.float32(0.0)
    ).astype(jnp.bfloat16)
    page_sum = jnp.sum(weights.astype(jnp.float32), axis=2)
    page_out = jnp.einsum(
        "pht,ptc->phc",
        weights,
        latent_cache[:, :, :latent_width],
        preferred_element_type=jnp.float32,
    )
    onehot = member.astype(jnp.float32)
    row_sum = jnp.dot(onehot, page_sum, precision=lax.Precision.HIGHEST)
    row_out = jnp.dot(
        onehot, page_out.reshape(pages_here, -1), precision=lax.Precision.HIGHEST
    ).reshape(row_count, -1, latent_width)
    tops = lax.all_to_all(row_top[None], "ctx", split_axis=2, concat_axis=0, tiled=True)
    sums = lax.all_to_all(row_sum[None], "ctx", split_axis=2, concat_axis=0, tiled=True)
    outs = lax.all_to_all(
        row_out[None].astype(jnp.bfloat16), "ctx", split_axis=2, concat_axis=0, tiled=True
    ).astype(jnp.float32)
    best = jnp.max(tops, axis=0)
    factor = jnp.exp(tops - best[None])
    merged_sum = jnp.sum(factor * sums, axis=0)
    merged_out = jnp.sum(factor[..., None] * outs, axis=0)
    partial_out = finish(merged_sum, merged_out, w_uv, w_out)
    return lax.psum(partial_out, "ctx").astype(jnp.bfloat16)


def partner(me, k):
    peer = 0
    for bit in (1, 2, 4):
        mine = (me // bit) % 2
        peer = peer + bit * ((1 - mine) if k & bit else mine)
    return peer


def pieces(value, count):
    terms = []
    for _ in range(count):
        term = value.astype(jnp.bfloat16).astype(jnp.float32)
        terms.append(term)
        value = value - term
    return terms


def kernel(
    ql_ref, qr_ref, cache_ref, table_hbm, len_hbm, uv_ref, wo_ref, out_ref,
    qall, rope, kv, states, got, uv, wo, part, parts, flat, table_ref, len_ref,
    local_sem, wo_sem, kv_send, kv_recv, q_send, q_recv, s_send, s_recv, p_send, p_recv,
):
    rows, heads, width = ql_ref.shape
    pages, page_len, key_width = cache_ref.shape
    tokens = 2 * pages * page_len
    slots = table_ref.shape[1]
    tiles = wo.shape[0]
    scale = (V + ROPE) ** (-0.5)
    me = lax.axis_index("ctx")
    peers = [partner(me, k) for k in range(N)]

    barrier = pltpu.get_barrier_semaphore()
    for k in SEND_ORDER:
        pl.semaphore_signal(
            barrier, inc=1, device_id={"ctx": peers[k]}, device_id_type=pl.DeviceIdType.MESH
        )

    load_ql = pltpu.make_async_copy(ql_ref, qall.at[0, :, :, pl.ds(0, width)], local_sem.at[0])
    load_qr = pltpu.make_async_copy(qr_ref, rope, local_sem.at[1])
    load_kv = pltpu.make_async_copy(cache_ref, kv.at[0], local_sem.at[2])
    load_uv = pltpu.make_async_copy(uv_ref, uv, local_sem.at[3])
    load_table = pltpu.make_async_copy(table_hbm, table_ref, local_sem.at[4])
    load_len = pltpu.make_async_copy(len_hbm, len_ref, local_sem.at[5])
    load_ql.start()
    load_qr.start()
    load_table.start()
    load_len.start()
    load_kv.start()

    def load_wo(j):
        return pltpu.make_async_copy(
            wo_ref.at[:, pl.ds(pl.multiple_of(j * TILE, TILE), TILE)], wo.at[j], wo_sem.at[j]
        )

    for j in range(EARLY):
        load_wo(j).start()

    def remote(src, dst, send, recv, k):
        return pltpu.make_async_remote_copy(
            src_ref=src, dst_ref=dst, send_sem=send, recv_sem=recv,
            device_id={"ctx": peers[k]}, device_id_type=pl.DeviceIdType.MESH,
        )

    def query_copy(e):
        return remote(qall.at[0], qall.at[e], q_send.at[e], q_recv.at[e], 2 * e)

    def state_copy(e):
        return remote(states.at[e], got.at[e], s_send.at[e], s_recv.at[e], 2 * e)

    swap = remote(kv.at[0], kv.at[1], kv_send, kv_recv, 1)

    load_ql.wait()
    load_qr.wait()
    qall[0, :, :, width:] = jnp.concatenate([rope[...], jnp.zeros_like(rope)], axis=2)
    load_kv.wait()
    pl.semaphore_wait(barrier, N - 1)
    swap.start()
    for e in CHIP_ORDER:
        query_copy(e).start()
    load_uv.start()
    for j in range(EARLY, tiles):
        load_wo(j).start()

    load_table.wait()
    load_len.wait()
    lane = lax.broadcasted_iota(jnp.int32, (1, tokens), 1)
    page = lane // page_len
    page = jnp.where(page < pages, page + me * pages, page + (peers[1] - 1) * pages)
    offset = lane % page_len
    live = []
    for r in range(rows):
        limit = jnp.zeros((1, tokens), jnp.int32)
        for j in range(slots):
            limit = jnp.where(page == table_ref[r, j], len_ref[r] - j * page_len, limit)
        live.append(offset < limit)

    block = rows * heads
    for group in GROUPS:
        for e in group:
            if e:
                query_copy(e).wait_recv()
        first, count = group[0], len(group)
        query = qall[first : first + count].reshape(count * block, width + LANES)[:, :key_width]
        halves = []
        for i in range(2):
            if i and group == GROUPS[0]:
                swap.wait_recv()
            halves.append(
                lax.dot_general(
                    query,
                    kv[i].reshape(tokens // 2, key_width),
                    (((1,), (1,)), ((), ())),
                    preferred_element_type=jnp.float32,
                )
            )
        scores = jnp.concatenate(halves, axis=1) * scale
        keys = kv[:, :, :, :width].reshape(tokens, width)
        scores = jnp.concatenate(
            [
                jnp.where(live[i % rows], scores[i * heads : (i + 1) * heads], jnp.float32(NEG))
                for i in range(count * rows)
            ],
            axis=0,
        )
        top = jnp.max(scores, axis=1, keepdims=True)
        weights = jnp.exp(scores - jnp.maximum(top, jnp.float32(FLOOR))).astype(jnp.bfloat16)
        total = jnp.sum(weights.astype(jnp.float32), axis=1, keepdims=True)
        summed = jnp.dot(weights, keys, preferred_element_type=jnp.float32)
        states[first : first + count, :, :, :width] = summed.astype(jnp.bfloat16).reshape(
            count, rows, heads, width
        )
        place = lax.broadcasted_iota(jnp.int32, (count * block, LANES), 1)
        stats = jnp.zeros((count * block, LANES), jnp.float32)
        for i, term in enumerate(pieces(top, 3) + pieces(total, 3)):
            stats = jnp.where(place == i, term, stats)
        states[first : first + count, :, :, width:] = stats.astype(jnp.bfloat16).reshape(
            count, rows, heads, LANES
        )
        for e in group:
            if e:
                state_copy(e).start()

    place = lax.broadcasted_iota(jnp.int32, (block, LANES), 1)
    tops, sums = [], []
    for e in range(CHIPS):
        if e:
            state_copy(e).wait_recv()
        source = got.at[e] if e else states.at[0]
        stats = source[:, :, width:].reshape(block, LANES).astype(jnp.float32)
        tops.append(jnp.sum(jnp.where(place < 3, stats, 0.0), axis=1, keepdims=True))
        sums.append(
            jnp.sum(jnp.where((place >= 3) & (place < 6), stats, 0.0), axis=1, keepdims=True)
        )
    best = functools.reduce(jnp.maximum, tops)
    merged = jnp.zeros((block, width), jnp.float32)
    merged_sum = jnp.zeros((block, 1), jnp.float32)
    for e in range(CHIPS):
        source = got.at[e] if e else states.at[0]
        factor = jnp.exp(tops[e] - best)
        merged_sum = merged_sum + factor * sums[e]
        merged = merged + factor * source[:, :, :width].reshape(block, width).astype(jnp.float32)
    latent = (merged / merged_sum).astype(jnp.bfloat16)

    load_uv.wait()
    for h in range(0, heads, 2):
        pair = jnp.concatenate([uv[h], uv[h + 1]], axis=1)
        product = jnp.dot(latent, pair, preferred_element_type=jnp.float32)
        for r in range(rows):
            for i in range(2):
                row = r * heads + h + i
                flat[r : r + 1, (h + i) * V : (h + i + 1) * V] = product[
                    row : row + 1, i * V : (i + 1) * V
                ]
    head_out = flat[...].astype(jnp.bfloat16)

    for begin, end in ((0, tiles - LATE), (tiles - LATE, tiles)):
        for j in range(begin, end):
            load_wo(j).wait()
            term = jnp.dot(head_out, wo[j], preferred_element_type=jnp.float32)
            dense = jnp.concatenate(
                [term[:, c * LANES : (c + 1) * LANES] for c in range(TILE // LANES)], axis=0
            )
            part[j] = dense.astype(jnp.bfloat16)
        some = pl.ds(begin, end - begin)
        for k in SEND_ORDER:
            remote(part.at[some], parts.at[k, some], p_send.at[k], p_recv.at[k], k).start()

    terms = []
    for k in range(N):
        if k:
            remote(part, parts.at[k], p_send.at[k], p_recv.at[k], k).wait_recv()
        terms.append((parts[k] if k else part[...]).astype(jnp.float32))
    while len(terms) > 1:
        terms = [terms[i] + terms[i + 1] for i in range(0, len(terms), 2)]
    total = terms[0]
    for j in range(tiles):
        for c in range(TILE // LANES):
            start = j * TILE + c * LANES
            out_ref[:, start : start + LANES] = total[j, c * rows : (c + 1) * rows, :]

    swap.wait_send()
    for e in CHIP_ORDER:
        query_copy(e).wait_send()
        state_copy(e).wait_send()
    for k in SEND_ORDER:
        remote(part, parts.at[k], p_send.at[k], p_recv.at[k], k).wait_send()


def fused(q_latent, q_rope, latent_cache, page_table, lengths, w_uv, w_out):
    rows, heads, width = q_latent.shape
    depth, columns = w_out.shape
    tiles = columns // TILE
    dense_rows = TILE // LANES * rows
    bf16 = jnp.bfloat16
    any_space = pl.BlockSpec(memory_space=pl.ANY)
    out = pl.pallas_call(
        kernel,
        out_shape=pltpu.VMEM((rows, columns), jnp.float32),
        in_specs=[any_space] * 7,
        out_specs=pl.BlockSpec(memory_space=pltpu.VMEM),
        scratch_shapes=[
            pltpu.VMEM((CHIPS, rows, heads, width + LANES), bf16),
            pltpu.VMEM(q_rope.shape, bf16),
            pltpu.VMEM((2,) + latent_cache.shape, bf16),
            pltpu.VMEM((CHIPS, rows, heads, width + LANES), bf16),
            pltpu.VMEM((CHIPS, rows, heads, width + LANES), bf16),
            pltpu.VMEM(w_uv.shape, bf16),
            pltpu.VMEM((tiles, depth, TILE), bf16),
            pltpu.VMEM((tiles, dense_rows, LANES), bf16),
            pltpu.VMEM((N, tiles, dense_rows, LANES), bf16),
            pltpu.VMEM((rows, depth), jnp.float32),
            pltpu.SMEM(page_table.shape, jnp.int32),
            pltpu.SMEM(lengths.shape, jnp.int32),
            pltpu.SemaphoreType.DMA((6,)),
            pltpu.SemaphoreType.DMA((tiles,)),
            pltpu.SemaphoreType.DMA,
            pltpu.SemaphoreType.DMA,
            pltpu.SemaphoreType.DMA((CHIPS,)),
            pltpu.SemaphoreType.DMA((CHIPS,)),
            pltpu.SemaphoreType.DMA((CHIPS,)),
            pltpu.SemaphoreType.DMA((CHIPS,)),
            pltpu.SemaphoreType.DMA((N,)),
            pltpu.SemaphoreType.DMA((N,)),
        ],
        compiler_params=pltpu.CompilerParams(
            collective_id=0, has_side_effects=True, vmem_limit_bytes=56 * 1024 * 1024
        ),
        cost_estimate=pl.CostEstimate(
            flops=2 * rows * depth * columns, bytes_accessed=2 * depth * columns, transcendentals=0
        ),
    )(q_latent, q_rope, latent_cache, page_table, lengths, w_uv, w_out)
    return out.astype(bf16)


def solution(mesh):
    in_specs = (
        P("grp", "ctx", None),
        P("grp", "ctx", None),
        P(("grp", "ctx"), None, None),
        P("grp", None),
        P("grp"),
        P("ctx", None, None),
        P("ctx", None),
    )
    out_specs = P("grp", None)

    def program(q_latent, q_rope, latent_cache, page_table, lengths, w_uv, w_out):
        rows, heads, width = q_latent.shape
        suits = (
            mesh.shape["ctx"] == N
            and rows * (TILE // LANES) == 16
            and heads % 16 == 0
            and width % LANES == 0
            and w_uv.shape[2] == V
            and w_out.shape[1] % TILE == 0
            and w_out.shape[1] > LATE * TILE
            and w_out.size * 2 <= 32 * 1024 * 1024
            and latent_cache.size * 2 <= 2 * 1024 * 1024
        )
        body = fused if suits else local
        return body(q_latent, q_rope, latent_cache, page_table, lengths, w_uv, w_out)

    return jax.shard_map(program, mesh=mesh, in_specs=in_specs, out_specs=out_specs, check_vma=False)
```

```python
import functools

import jax
import jax.numpy as jnp
from jax import lax
from jax.experimental import pallas as pl
from jax.experimental.pallas import tpu as pltpu
from jax.sharding import PartitionSpec as P

ROPE = 64
V = 128


NEG = -1e30
FLOOR = -1e29
N = 8
TILE = 1024
LANES = 128
CHIPS = 4
GROUPS = ((1, 2, 3), (0,))
LATE = 2
CHIP_ORDER = (3, 1, 2)
SEND_ORDER = (6, 7, 2, 4, 3, 5, 1)


def finish(row_sums, row_outs, w_uv, w_out):
    latent = (row_outs / row_sums[..., None]).astype(jnp.bfloat16)
    head_out = jnp.einsum("rhc,hcv->rhv", latent, w_uv, preferred_element_type=jnp.float32).astype(
        jnp.bfloat16
    )
    flat = head_out.reshape(head_out.shape[0], -1)
    return jnp.dot(flat, w_out, preferred_element_type=jnp.float32)


def local(q_latent, q_rope, latent_cache, page_table, lengths, w_uv, w_out):
    score_scale = (V + ROPE) ** (-0.5)
    local_query = jnp.concatenate([q_latent, q_rope], axis=2)
    all_query = lax.all_gather(local_query, "ctx", axis=1, tiled=True)
    pages_here = latent_cache.shape[0]
    page_len = latent_cache.shape[1]
    row_count = page_table.shape[0]
    slot_width = page_table.shape[1]
    slot_count = row_count * slot_width
    latent_width = q_latent.shape[2]
    inverse = (
        jnp.zeros((slot_count,), jnp.int32)
        .at[page_table.reshape(-1)]
        .set(jnp.arange(slot_count, dtype=jnp.int32))
    )
    first_page = lax.axis_index("ctx") * pages_here
    slot_ids = lax.dynamic_slice_in_dim(inverse, first_page, pages_here)
    owner_row = slot_ids // slot_width
    logical = slot_ids % slot_width
    page_query = all_query[owner_row]
    scores = (
        jnp.einsum("phc,ptc->pht", page_query, latent_cache, preferred_element_type=jnp.float32)
        * score_scale
    )
    position = logical[:, None] * page_len + jnp.arange(page_len, dtype=jnp.int32)[None, :]
    live_mask = position < lengths[owner_row][:, None]
    scores = jnp.where(live_mask[:, None, :], scores, jnp.float32(NEG))
    page_top = jnp.max(scores, axis=2)
    member = owner_row[None, :] == jnp.arange(row_count, dtype=jnp.int32)[:, None]
    row_top = jnp.max(jnp.where(member[:, :, None], page_top[None, :, :], jnp.float32(NEG)), axis=1)
    row_shift = row_top[owner_row]
    weights = jnp.where(
        live_mask[:, None, :], jnp.exp(scores - row_shift[:, :, None]), jnp.float32(0.0)
    ).astype(jnp.bfloat16)
    page_sum = jnp.sum(weights.astype(jnp.float32), axis=2)
    page_out = jnp.einsum(
        "pht,ptc->phc",
        weights,
        latent_cache[:, :, :latent_width],
        preferred_element_type=jnp.float32,
    )
    onehot = member.astype(jnp.float32)
    row_sum = jnp.dot(onehot, page_sum, precision=lax.Precision.HIGHEST)
    row_out = jnp.dot(
        onehot, page_out.reshape(pages_here, -1), precision=lax.Precision.HIGHEST
    ).reshape(row_count, -1, latent_width)
    tops = lax.all_to_all(row_top[None], "ctx", split_axis=2, concat_axis=0, tiled=True)
    sums = lax.all_to_all(row_sum[None], "ctx", split_axis=2, concat_axis=0, tiled=True)
    outs = lax.all_to_all(
        row_out[None].astype(jnp.bfloat16), "ctx", split_axis=2, concat_axis=0, tiled=True
    ).astype(jnp.float32)
    best = jnp.max(tops, axis=0)
    factor = jnp.exp(tops - best[None])
    merged_sum = jnp.sum(factor * sums, axis=0)
    merged_out = jnp.sum(factor[..., None] * outs, axis=0)
    partial_out = finish(merged_sum, merged_out, w_uv, w_out)
    return lax.psum(partial_out, "ctx").astype(jnp.bfloat16)


def partner(me, k):
    peer = 0
    for bit in (1, 2, 4):
        mine = (me // bit) % 2
        peer = peer + bit * ((1 - mine) if k & bit else mine)
    return peer


def pieces(value, count):
    terms = []
    for _ in range(count):
        term = value.astype(jnp.bfloat16).astype(jnp.float32)
        terms.append(term)
        value = value - term
    return terms


def kernel(
    ql_ref, qr_ref, cache_ref, table_hbm, len_hbm, uv_ref, wo_ref, out_ref,
    qall, rope, kv, states, got, uv, wo, part, parts, flat, dense, table_ref, len_ref,
    local_sem, wo_sem, kv_send, kv_recv, q_send, q_recv, s_send, s_recv, p_send, p_recv,
):
    rows, heads, width = ql_ref.shape
    pages, page_len, key_width = cache_ref.shape
    tokens = 2 * pages * page_len
    slots = table_ref.shape[1]
    tiles = wo.shape[0]
    scale = (V + ROPE) ** (-0.5)
    me = lax.axis_index("ctx")
    peers = [partner(me, k) for k in range(N)]

    barrier = pltpu.get_barrier_semaphore()
    for k in SEND_ORDER:
        pl.semaphore_signal(
            barrier, inc=1, device_id={"ctx": peers[k]}, device_id_type=pl.DeviceIdType.MESH
        )

    load_ql = pltpu.make_async_copy(ql_ref, qall.at[0, :, :, pl.ds(0, width)], local_sem.at[0])
    load_qr = pltpu.make_async_copy(qr_ref, rope, local_sem.at[1])
    load_kv = pltpu.make_async_copy(cache_ref, kv.at[0], local_sem.at[2])
    load_uv = pltpu.make_async_copy(uv_ref, uv, local_sem.at[3])
    load_table = pltpu.make_async_copy(table_hbm, table_ref, local_sem.at[4])
    load_len = pltpu.make_async_copy(len_hbm, len_ref, local_sem.at[5])
    load_ql.start()
    load_qr.start()
    load_table.start()
    load_len.start()
    load_kv.start()

    def load_wo(j):
        return pltpu.make_async_copy(
            wo_ref.at[:, pl.ds(pl.multiple_of(j * TILE, TILE), TILE)], wo.at[j], wo_sem.at[j]
        )

    def remote(src, dst, send, recv, k):
        return pltpu.make_async_remote_copy(
            src_ref=src, dst_ref=dst, send_sem=send, recv_sem=recv,
            device_id={"ctx": peers[k]}, device_id_type=pl.DeviceIdType.MESH,
        )

    def query_copy(e):
        return remote(qall.at[0], qall.at[e], q_send.at[e], q_recv.at[e], 2 * e)

    def state_copy(e):
        return remote(states.at[e], got.at[e], s_send.at[e], s_recv.at[e], 2 * e)

    swap = remote(kv.at[0], kv.at[1], kv_send, kv_recv, 1)

    load_ql.wait()
    load_qr.wait()
    qall[0, :, :, width:] = jnp.concatenate([rope[...], jnp.zeros_like(rope)], axis=2)
    load_kv.wait()
    pl.semaphore_wait(barrier, N - 1)
    swap.start()
    for e in CHIP_ORDER:
        query_copy(e).start()
    load_uv.start()
    for j in range(tiles):
        load_wo(j).start()

    load_table.wait()
    load_len.wait()
    lane = lax.broadcasted_iota(jnp.int32, (1, tokens), 1)
    page = lane // page_len
    page = jnp.where(page < pages, page + me * pages, page + (peers[1] - 1) * pages)
    offset = lane % page_len
    live = []
    for r in range(rows):
        limit = jnp.zeros((1, tokens), jnp.int32)
        for j in range(slots):
            limit = jnp.where(page == table_ref[r, j], len_ref[r] - j * page_len, limit)
        live.append(offset < limit)

    block = rows * heads
    for group in GROUPS:
        for e in group:
            if e:
                query_copy(e).wait_recv()
        first, count = group[0], len(group)
        query = qall[first : first + count].reshape(count * block, width + LANES)[:, :key_width]
        halves = []
        for i in range(2):
            if i and group == GROUPS[0]:
                swap.wait_recv()
            halves.append(
                lax.dot_general(
                    query,
                    kv[i].reshape(tokens // 2, key_width),
                    (((1,), (1,)), ((), ())),
                    preferred_element_type=jnp.float32,
                )
            )
        scores = jnp.concatenate(halves, axis=1) * scale
        keys = kv[:, :, :, :width].reshape(tokens, width)
        scores = jnp.concatenate(
            [
                jnp.where(live[i % rows], scores[i * heads : (i + 1) * heads], jnp.float32(NEG))
                for i in range(count * rows)
            ],
            axis=0,
        )
        top = jnp.max(scores, axis=1, keepdims=True)
        weights = jnp.exp(scores - jnp.maximum(top, jnp.float32(FLOOR))).astype(jnp.bfloat16)
        total = jnp.sum(weights.astype(jnp.float32), axis=1, keepdims=True)
        summed = jnp.dot(weights, keys, preferred_element_type=jnp.float32)
        states[first : first + count, :, :, :width] = summed.astype(jnp.bfloat16).reshape(
            count, rows, heads, width
        )
        place = lax.broadcasted_iota(jnp.int32, (count * block, LANES), 1)
        stats = jnp.zeros((count * block, LANES), jnp.float32)
        for i, term in enumerate(pieces(top, 3) + pieces(total, 3)):
            stats = jnp.where(place == i, term, stats)
        states[first : first + count, :, :, width:] = stats.astype(jnp.bfloat16).reshape(
            count, rows, heads, LANES
        )
        for e in group:
            if e:
                state_copy(e).start()

    place = lax.broadcasted_iota(jnp.int32, (block, LANES), 1)
    tops, sums = [], []
    for e in range(CHIPS):
        if e:
            state_copy(e).wait_recv()
        source = got.at[e] if e else states.at[0]
        stats = source[:, :, width:].reshape(block, LANES).astype(jnp.float32)
        tops.append(jnp.sum(jnp.where(place < 3, stats, 0.0), axis=1, keepdims=True))
        sums.append(
            jnp.sum(jnp.where((place >= 3) & (place < 6), stats, 0.0), axis=1, keepdims=True)
        )
    best = functools.reduce(jnp.maximum, tops)
    merged = jnp.zeros((block, width), jnp.float32)
    merged_sum = jnp.zeros((block, 1), jnp.float32)
    for e in range(CHIPS):
        source = got.at[e] if e else states.at[0]
        factor = jnp.exp(tops[e] - best)
        merged_sum = merged_sum + factor * sums[e]
        merged = merged + factor * source[:, :, :width].reshape(block, width).astype(jnp.float32)
    latent = (merged / merged_sum).astype(jnp.bfloat16)

    load_uv.wait()
    for h in range(0, heads, 2):
        pair = jnp.concatenate([uv[h], uv[h + 1]], axis=1)
        product = jnp.dot(latent, pair, preferred_element_type=jnp.float32)
        for r in range(rows):
            for i in range(2):
                row = r * heads + h + i
                flat[r : r + 1, (h + i) * V : (h + i + 1) * V] = product[
                    row : row + 1, i * V : (i + 1) * V
                ]
    head_out = flat[...].astype(jnp.bfloat16)

    def step(j, carry):
        load_wo(j).wait()
        term = jnp.dot(head_out, wo[j], preferred_element_type=jnp.float32)
        for c in range(TILE // LANES):
            dense[c * rows : (c + 1) * rows, :] = term[:, c * LANES : (c + 1) * LANES]
        part[j] = dense[...].astype(jnp.bfloat16)
        return carry

    for begin, end in ((0, tiles - LATE), (tiles - LATE, tiles)):
        lax.fori_loop(begin, end, step, 0)
        some = pl.ds(begin, end - begin)
        for k in SEND_ORDER:
            remote(part.at[some], parts.at[k, some], p_send.at[k], p_recv.at[k], k).start()

    terms = []
    for k in range(N):
        if k:
            remote(part, parts.at[k], p_send.at[k], p_recv.at[k], k).wait_recv()
        terms.append((parts[k] if k else part[...]).astype(jnp.float32))
    while len(terms) > 1:
        terms = [terms[i] + terms[i + 1] for i in range(0, len(terms), 2)]
    total = terms[0]
    for j in range(tiles):
        for c in range(TILE // LANES):
            start = j * TILE + c * LANES
            out_ref[:, start : start + LANES] = total[j, c * rows : (c + 1) * rows, :]

    swap.wait_send()
    for e in CHIP_ORDER:
        query_copy(e).wait_send()
        state_copy(e).wait_send()
    for k in SEND_ORDER:
        remote(part, parts.at[k], p_send.at[k], p_recv.at[k], k).wait_send()


def fused(q_latent, q_rope, latent_cache, page_table, lengths, w_uv, w_out):
    rows, heads, width = q_latent.shape
    depth, columns = w_out.shape
    tiles = columns // TILE
    dense_rows = TILE // LANES * rows
    bf16 = jnp.bfloat16
    any_space = pl.BlockSpec(memory_space=pl.ANY)
    out = pl.pallas_call(
        kernel,
        out_shape=pltpu.VMEM((rows, columns), jnp.float32),
        in_specs=[any_space] * 7,
        out_specs=pl.BlockSpec(memory_space=pltpu.VMEM),
        scratch_shapes=[
            pltpu.VMEM((CHIPS, rows, heads, width + LANES), bf16),
            pltpu.VMEM(q_rope.shape, bf16),
            pltpu.VMEM((2,) + latent_cache.shape, bf16),
            pltpu.VMEM((CHIPS, rows, heads, width + LANES), bf16),
            pltpu.VMEM((CHIPS, rows, heads, width + LANES), bf16),
            pltpu.VMEM(w_uv.shape, bf16),
            pltpu.VMEM((tiles, depth, TILE), bf16),
            pltpu.VMEM((tiles, dense_rows, LANES), bf16),
            pltpu.VMEM((N, tiles, dense_rows, LANES), bf16),
            pltpu.VMEM((rows, depth), jnp.float32),
            pltpu.VMEM((dense_rows, LANES), jnp.float32),
            pltpu.SMEM(page_table.shape, jnp.int32),
            pltpu.SMEM(lengths.shape, jnp.int32),
            pltpu.SemaphoreType.DMA((6,)),
            pltpu.SemaphoreType.DMA((tiles,)),
            pltpu.SemaphoreType.DMA,
            pltpu.SemaphoreType.DMA,
            pltpu.SemaphoreType.DMA((CHIPS,)),
            pltpu.SemaphoreType.DMA((CHIPS,)),
            pltpu.SemaphoreType.DMA((CHIPS,)),
            pltpu.SemaphoreType.DMA((CHIPS,)),
            pltpu.SemaphoreType.DMA((N,)),
            pltpu.SemaphoreType.DMA((N,)),
        ],
        compiler_params=pltpu.CompilerParams(
            collective_id=0, has_side_effects=True, vmem_limit_bytes=56 * 1024 * 1024
        ),
        cost_estimate=pl.CostEstimate(
            flops=2 * rows * depth * columns, bytes_accessed=2 * depth * columns, transcendentals=0
        ),
    )(q_latent, q_rope, latent_cache, page_table, lengths, w_uv, w_out)
    return out.astype(bf16)


def solution(mesh):
    in_specs = (
        P("grp", "ctx", None),
        P("grp", "ctx", None),
        P(("grp", "ctx"), None, None),
        P("grp", None),
        P("grp"),
        P("ctx", None, None),
        P("ctx", None),
    )
    out_specs = P("grp", None)

    def program(q_latent, q_rope, latent_cache, page_table, lengths, w_uv, w_out):
        rows, heads, width = q_latent.shape
        suits = (
            mesh.shape["ctx"] == N
            and rows * (TILE // LANES) == 16
            and heads % 16 == 0
            and width % LANES == 0
            and w_uv.shape[2] == V
            and w_out.shape[1] % TILE == 0
            and w_out.shape[1] > LATE * TILE
            and w_out.size * 2 <= 32 * 1024 * 1024
            and latent_cache.size * 2 <= 2 * 1024 * 1024
        )
        body = fused if suits else local
        return body(q_latent, q_rope, latent_cache, page_table, lengths, w_uv, w_out)

    return jax.shard_map(program, mesh=mesh, in_specs=in_specs, out_specs=out_specs, check_vma=False)
```

```python
import functools

import jax
import jax.numpy as jnp
from jax import lax
from jax.experimental import pallas as pl
from jax.experimental.pallas import tpu as pltpu
from jax.sharding import PartitionSpec as P

ROPE = 64
V = 128


NEG = -1e30
FLOOR = -1e29
N = 8
TILE = 1024
LANES = 128
CHIPS = 4
GROUPS = ((1, 2, 3), (0,))
EARLY = 2
LATE = 2
CHIP_ORDER = (3, 1, 2)
SEND_ORDER = (6, 7, 2, 4, 3, 5, 1)


def finish(row_sums, row_outs, w_uv, w_out):
    latent = (row_outs / row_sums[..., None]).astype(jnp.bfloat16)
    head_out = jnp.einsum("rhc,hcv->rhv", latent, w_uv, preferred_element_type=jnp.float32).astype(
        jnp.bfloat16
    )
    flat = head_out.reshape(head_out.shape[0], -1)
    return jnp.dot(flat, w_out, preferred_element_type=jnp.float32)


def local(q_latent, q_rope, latent_cache, page_table, lengths, w_uv, w_out):
    score_scale = (V + ROPE) ** (-0.5)
    local_query = jnp.concatenate([q_latent, q_rope], axis=2)
    all_query = lax.all_gather(local_query, "ctx", axis=1, tiled=True)
    pages_here = latent_cache.shape[0]
    page_len = latent_cache.shape[1]
    row_count = page_table.shape[0]
    slot_width = page_table.shape[1]
    slot_count = row_count * slot_width
    latent_width = q_latent.shape[2]
    inverse = (
        jnp.zeros((slot_count,), jnp.int32)
        .at[page_table.reshape(-1)]
        .set(jnp.arange(slot_count, dtype=jnp.int32))
    )
    first_page = lax.axis_index("ctx") * pages_here
    slot_ids = lax.dynamic_slice_in_dim(inverse, first_page, pages_here)
    owner_row = slot_ids // slot_width
    logical = slot_ids % slot_width
    page_query = all_query[owner_row]
    scores = (
        jnp.einsum("phc,ptc->pht", page_query, latent_cache, preferred_element_type=jnp.float32)
        * score_scale
    )
    position = logical[:, None] * page_len + jnp.arange(page_len, dtype=jnp.int32)[None, :]
    live_mask = position < lengths[owner_row][:, None]
    scores = jnp.where(live_mask[:, None, :], scores, jnp.float32(NEG))
    page_top = jnp.max(scores, axis=2)
    member = owner_row[None, :] == jnp.arange(row_count, dtype=jnp.int32)[:, None]
    row_top = jnp.max(jnp.where(member[:, :, None], page_top[None, :, :], jnp.float32(NEG)), axis=1)
    row_shift = row_top[owner_row]
    weights = jnp.where(
        live_mask[:, None, :], jnp.exp(scores - row_shift[:, :, None]), jnp.float32(0.0)
    ).astype(jnp.bfloat16)
    page_sum = jnp.sum(weights.astype(jnp.float32), axis=2)
    page_out = jnp.einsum(
        "pht,ptc->phc",
        weights,
        latent_cache[:, :, :latent_width],
        preferred_element_type=jnp.float32,
    )
    onehot = member.astype(jnp.float32)
    row_sum = jnp.dot(onehot, page_sum, precision=lax.Precision.HIGHEST)
    row_out = jnp.dot(
        onehot, page_out.reshape(pages_here, -1), precision=lax.Precision.HIGHEST
    ).reshape(row_count, -1, latent_width)
    tops = lax.all_to_all(row_top[None], "ctx", split_axis=2, concat_axis=0, tiled=True)
    sums = lax.all_to_all(row_sum[None], "ctx", split_axis=2, concat_axis=0, tiled=True)
    outs = lax.all_to_all(
        row_out[None].astype(jnp.bfloat16), "ctx", split_axis=2, concat_axis=0, tiled=True
    ).astype(jnp.float32)
    best = jnp.max(tops, axis=0)
    factor = jnp.exp(tops - best[None])
    merged_sum = jnp.sum(factor * sums, axis=0)
    merged_out = jnp.sum(factor[..., None] * outs, axis=0)
    partial_out = finish(merged_sum, merged_out, w_uv, w_out)
    return lax.psum(partial_out, "ctx").astype(jnp.bfloat16)


def partner(me, k):
    peer = 0
    for bit in (1, 2, 4):
        mine = (me // bit) % 2
        peer = peer + bit * ((1 - mine) if k & bit else mine)
    return peer


def pieces(value, count):
    terms = []
    for _ in range(count):
        term = value.astype(jnp.bfloat16).astype(jnp.float32)
        terms.append(term)
        value = value - term
    return terms


def kernel(
    ql_ref, qr_ref, cache_ref, table_hbm, len_hbm, uv_ref, wo_ref, out_ref,
    qall, rope, kv, states, got, uv, wo, part, parts, flat, dense, table_ref, len_ref,
    local_sem, wo_sem, kv_send, kv_recv, q_send, q_recv, s_send, s_recv, p_send, p_recv,
):
    rows, heads, width = ql_ref.shape
    pages, page_len, key_width = cache_ref.shape
    tokens = 2 * pages * page_len
    slots = table_ref.shape[1]
    tiles = wo.shape[0]
    scale = (V + ROPE) ** (-0.5)
    me = lax.axis_index("ctx")
    peers = [partner(me, k) for k in range(N)]

    barrier = pltpu.get_barrier_semaphore()
    for k in SEND_ORDER:
        pl.semaphore_signal(
            barrier, inc=1, device_id={"ctx": peers[k]}, device_id_type=pl.DeviceIdType.MESH
        )

    load_ql = pltpu.make_async_copy(ql_ref, qall.at[0, :, :, pl.ds(0, width)], local_sem.at[0])
    load_qr = pltpu.make_async_copy(qr_ref, rope, local_sem.at[1])
    load_kv = pltpu.make_async_copy(cache_ref, kv.at[0], local_sem.at[2])
    load_uv = pltpu.make_async_copy(uv_ref, uv, local_sem.at[3])
    load_table = pltpu.make_async_copy(table_hbm, table_ref, local_sem.at[4])
    load_len = pltpu.make_async_copy(len_hbm, len_ref, local_sem.at[5])
    load_ql.start()
    load_qr.start()
    load_table.start()
    load_len.start()
    load_kv.start()

    def load_wo(j):
        return pltpu.make_async_copy(
            wo_ref.at[:, pl.ds(pl.multiple_of(j * TILE, TILE), TILE)], wo.at[j], wo_sem.at[j]
        )

    def remote(src, dst, send, recv, k):
        return pltpu.make_async_remote_copy(
            src_ref=src, dst_ref=dst, send_sem=send, recv_sem=recv,
            device_id={"ctx": peers[k]}, device_id_type=pl.DeviceIdType.MESH,
        )

    def query_copy(e):
        return remote(qall.at[0], qall.at[e], q_send.at[e], q_recv.at[e], 2 * e)

    def state_copy(e):
        return remote(states.at[e], got.at[e], s_send.at[e], s_recv.at[e], 2 * e)

    swap = remote(kv.at[0], kv.at[1], kv_send, kv_recv, 1)

    load_ql.wait()
    load_qr.wait()
    qall[0, :, :, width:] = jnp.concatenate([rope[...], jnp.zeros_like(rope)], axis=2)
    load_kv.wait()
    pl.semaphore_wait(barrier, N - 1)
    swap.start()
    for e in CHIP_ORDER:
        query_copy(e).start()
    for j in range(EARLY):
        load_wo(j).start()

    load_table.wait()
    load_len.wait()
    lane = lax.broadcasted_iota(jnp.int32, (1, tokens), 1)
    page = lane // page_len
    page = jnp.where(page < pages, page + me * pages, page + (peers[1] - 1) * pages)
    offset = lane % page_len
    live = []
    for r in range(rows):
        limit = jnp.zeros((1, tokens), jnp.int32)
        for j in range(slots):
            limit = jnp.where(page == table_ref[r, j], len_ref[r] - j * page_len, limit)
        live.append(offset < limit)

    swap.wait_recv()
    keys = kv[...].reshape(tokens, key_width)
    block = rows * heads
    for group in GROUPS:
        for e in group:
            if e:
                query_copy(e).wait_recv()
        first, count = group[0], len(group)
        query = qall[first : first + count].reshape(count * block, width + LANES)[:, :key_width]
        scores = (
            lax.dot_general(
                query, keys, (((1,), (1,)), ((), ())), preferred_element_type=jnp.float32
            )
            * scale
        )
        scores = jnp.concatenate(
            [
                jnp.where(live[i % rows], scores[i * heads : (i + 1) * heads], jnp.float32(NEG))
                for i in range(count * rows)
            ],
            axis=0,
        )
        top = jnp.max(scores, axis=1, keepdims=True)
        weights = jnp.exp(scores - jnp.maximum(top, jnp.float32(FLOOR))).astype(jnp.bfloat16)
        total = jnp.sum(weights.astype(jnp.float32), axis=1, keepdims=True)
        summed = jnp.dot(weights, keys[:, :width], preferred_element_type=jnp.float32)
        states[first : first + count, :, :, :width] = summed.astype(jnp.bfloat16).reshape(
            count, rows, heads, width
        )
        place = lax.broadcasted_iota(jnp.int32, (count * block, LANES), 1)
        stats = jnp.zeros((count * block, LANES), jnp.float32)
        for i, term in enumerate(pieces(top, 3) + pieces(total, 3)):
            stats = jnp.where(place == i, term, stats)
        states[first : first + count, :, :, width:] = stats.astype(jnp.bfloat16).reshape(
            count, rows, heads, LANES
        )
        for e in group:
            if e:
                state_copy(e).start()
        if group == GROUPS[0]:
            load_uv.start()
            for j in range(EARLY, tiles):
                load_wo(j).start()

    place = lax.broadcasted_iota(jnp.int32, (block, LANES), 1)
    tops, sums = [], []
    for e in range(CHIPS):
        if e:
            state_copy(e).wait_recv()
        source = got.at[e] if e else states.at[0]
        stats = source[:, :, width:].reshape(block, LANES).astype(jnp.float32)
        tops.append(jnp.sum(jnp.where(place < 3, stats, 0.0), axis=1, keepdims=True))
        sums.append(
            jnp.sum(jnp.where((place >= 3) & (place < 6), stats, 0.0), axis=1, keepdims=True)
        )
    best = functools.reduce(jnp.maximum, tops)
    merged = jnp.zeros((block, width), jnp.float32)
    merged_sum = jnp.zeros((block, 1), jnp.float32)
    for e in range(CHIPS):
        source = got.at[e] if e else states.at[0]
        factor = jnp.exp(tops[e] - best)
        merged_sum = merged_sum + factor * sums[e]
        merged = merged + factor * source[:, :, :width].reshape(block, width).astype(jnp.float32)
    latent = (merged / merged_sum).astype(jnp.bfloat16)

    load_uv.wait()
    for h in range(0, heads, 2):
        pair = jnp.concatenate([uv[h], uv[h + 1]], axis=1)
        product = jnp.dot(latent, pair, preferred_element_type=jnp.float32)
        for r in range(rows):
            for i in range(2):
                row = r * heads + h + i
                flat[r : r + 1, (h + i) * V : (h + i + 1) * V] = product[
                    row : row + 1, i * V : (i + 1) * V
                ]
    head_out = flat[...].astype(jnp.bfloat16)

    def step(j, carry):
        load_wo(j).wait()
        term = jnp.dot(head_out, wo[j], preferred_element_type=jnp.float32)
        for c in range(TILE // LANES):
            dense[c * rows : (c + 1) * rows, :] = term[:, c * LANES : (c + 1) * LANES]
        part[j] = dense[...].astype(jnp.bfloat16)
        return carry

    for begin, end in ((0, tiles - LATE), (tiles - LATE, tiles)):
        lax.fori_loop(begin, end, step, 0)
        some = pl.ds(begin, end - begin)
        for k in SEND_ORDER:
            remote(part.at[some], parts.at[k, some], p_send.at[k], p_recv.at[k], k).start()

    terms = []
    for k in range(N):
        if k:
            remote(part, parts.at[k], p_send.at[k], p_recv.at[k], k).wait_recv()
        terms.append((parts[k] if k else part[...]).astype(jnp.float32))
    while len(terms) > 1:
        terms = [terms[i] + terms[i + 1] for i in range(0, len(terms), 2)]
    total = terms[0]
    for j in range(tiles):
        for c in range(TILE // LANES):
            start = j * TILE + c * LANES
            out_ref[:, start : start + LANES] = total[j, c * rows : (c + 1) * rows, :]

    swap.wait_send()
    for e in CHIP_ORDER:
        query_copy(e).wait_send()
        state_copy(e).wait_send()
    for k in SEND_ORDER:
        remote(part, parts.at[k], p_send.at[k], p_recv.at[k], k).wait_send()


def fused(q_latent, q_rope, latent_cache, page_table, lengths, w_uv, w_out):
    rows, heads, width = q_latent.shape
    depth, columns = w_out.shape
    tiles = columns // TILE
    dense_rows = TILE // LANES * rows
    bf16 = jnp.bfloat16
    any_space = pl.BlockSpec(memory_space=pl.ANY)
    out = pl.pallas_call(
        kernel,
        out_shape=pltpu.VMEM((rows, columns), jnp.float32),
        in_specs=[any_space] * 7,
        out_specs=pl.BlockSpec(memory_space=pltpu.VMEM),
        scratch_shapes=[
            pltpu.VMEM((CHIPS, rows, heads, width + LANES), bf16),
            pltpu.VMEM(q_rope.shape, bf16),
            pltpu.VMEM((2,) + latent_cache.shape, bf16),
            pltpu.VMEM((CHIPS, rows, heads, width + LANES), bf16),
            pltpu.VMEM((CHIPS, rows, heads, width + LANES), bf16),
            pltpu.VMEM(w_uv.shape, bf16),
            pltpu.VMEM((tiles, depth, TILE), bf16),
            pltpu.VMEM((tiles, dense_rows, LANES), bf16),
            pltpu.VMEM((N, tiles, dense_rows, LANES), bf16),
            pltpu.VMEM((rows, depth), jnp.float32),
            pltpu.VMEM((dense_rows, LANES), jnp.float32),
            pltpu.SMEM(page_table.shape, jnp.int32),
            pltpu.SMEM(lengths.shape, jnp.int32),
            pltpu.SemaphoreType.DMA((6,)),
            pltpu.SemaphoreType.DMA((tiles,)),
            pltpu.SemaphoreType.DMA,
            pltpu.SemaphoreType.DMA,
            pltpu.SemaphoreType.DMA((CHIPS,)),
            pltpu.SemaphoreType.DMA((CHIPS,)),
            pltpu.SemaphoreType.DMA((CHIPS,)),
            pltpu.SemaphoreType.DMA((CHIPS,)),
            pltpu.SemaphoreType.DMA((N,)),
            pltpu.SemaphoreType.DMA((N,)),
        ],
        compiler_params=pltpu.CompilerParams(
            collective_id=0, has_side_effects=True, vmem_limit_bytes=56 * 1024 * 1024
        ),
        cost_estimate=pl.CostEstimate(
            flops=2 * rows * depth * columns, bytes_accessed=2 * depth * columns, transcendentals=0
        ),
    )(q_latent, q_rope, latent_cache, page_table, lengths, w_uv, w_out)
    return out.astype(bf16)


def solution(mesh):
    in_specs = (
        P("grp", "ctx", None),
        P("grp", "ctx", None),
        P(("grp", "ctx"), None, None),
        P("grp", None),
        P("grp"),
        P("ctx", None, None),
        P("ctx", None),
    )
    out_specs = P("grp", None)

    def program(q_latent, q_rope, latent_cache, page_table, lengths, w_uv, w_out):
        rows, heads, width = q_latent.shape
        suits = (
            mesh.shape["ctx"] == N
            and rows * (TILE // LANES) == 16
            and heads % 16 == 0
            and width % LANES == 0
            and w_uv.shape[2] == V
            and w_out.shape[1] % TILE == 0
            and w_out.shape[1] > LATE * TILE
            and w_out.size * 2 <= 32 * 1024 * 1024
            and latent_cache.size * 2 <= 2 * 1024 * 1024
        )
        body = fused if suits else local
        return body(q_latent, q_rope, latent_cache, page_table, lengths, w_uv, w_out)

    return jax.shard_map(program, mesh=mesh, in_specs=in_specs, out_specs=out_specs, check_vma=False)
```
